32 devices in a mesh: wide: 8 (over z, x), act: 4 (over y, core).
Axes of the slice: x: 2, y: 2, z: 4, core: 2. Of those that a mesh axis runs over, the one named last changes fastest.
Arguments:
- prefix_rows: bfloat16 [81920, 2048], P(('wide', 'act')), may hold values from -6 to 6
- item_lengths: int32 [8, 16], P('wide'), may hold values from 1 to 1024, 10240 in all within a row
- action_stretch: float32 [128, 50, 32], P(('wide', 'act')), may hold values from -6 to 6
- flow_noise: float32 [128, 50, 32], P(('wide', 'act')), may hold values from -6 to 6
- flow_times: float32 [128], P(('wide', 'act')), may hold values from 0.05 to 1
- action_dims: int32 [128], P(('wide', 'act')), may hold values from 7 to 18
- norm_gains: float32 [5120], P(('wide', 'act')), may hold values from 0.5 to 1.5
- norm_gains_first: float32 [5120], P(('wide', 'act')), may hold values from -1.9073486e-05 to 1.9073486e-05
- norm_gains_second: float32 [5120], P(('wide', 'act')), may hold values from 7.0198023e-12 to 2.8619194e-11
- prefix_kv: float32 [2048, 512], P(('wide', 'act')), may hold values from -0.125 to 0.125
- prefix_kv_first: float32 [2048, 512], P(('wide', 'act')), may hold values from -1.9073486e-06 to 1.9073486e-06
- prefix_kv_second: float32 [2048, 512], P(('wide', 'act')), may hold values from 7.0198025e-14 to 2.8619194e-13
- action_in: float32 [128, 1024], P(('wide', 'act')), may hold values from -0.5 to 0.5
- action_in_first: float32 [128, 1024], P(('wide', 'act')), may hold values from -1.9073486e-06 to 1.9073486e-06
- action_in_second: float32 [128, 1024], P(('wide', 'act')), may hold values from 7.0198025e-14 to 2.8619194e-13
- action_qkv: float32 [1024, 2560], P(('wide', 'act')), may hold values from -0.1875 to 0.1875
- action_qkv_first: float32 [1024, 2560], P(('wide', 'act')), may hold values from -1.9073486e-06 to 1.9073486e-06
- action_qkv_second: float32 [1024, 2560], P(('wide', 'act')), may hold values from 7.0198025e-14 to 2.8619194e-13
- attn_out: float32 [2048, 1024], P(('wide', 'act')), may hold values from -0.5 to 0.5
- attn_out_first: float32 [2048, 1024], P(('wide', 'act')), may hold values from -1.9073486e-06 to 1.9073486e-06
- attn_out_second: float32 [2048, 1024], P(('wide', 'act')), may hold values from 7.0198025e-14 to 2.8619194e-13
- action_gate_up: float32 [1024, 8192], P(('wide', 'act')), may hold values from -0.1875 to 0.1875
- action_gate_up_first: float32 [1024, 8192], P(('wide', 'act')), may hold values from -1.9073486e-06 to 1.9073486e-06
- action_gate_up_second: float32 [1024, 8192], P(('wide', 'act')), may hold values from 7.0198025e-14 to 2.8619194e-13
- action_down: float32 [4096, 1024], P(('wide', 'act')), may hold values from -0.09375 to 0.09375
- action_down_first: float32 [4096, 1024], P(('wide', 'act')), may hold values from -1.9073486e-06 to 1.9073486e-06
- action_down_second: float32 [4096, 1024], P(('wide', 'act')), may hold values from 7.0198025e-14 to 2.8619194e-13
- action_head: float32 [1024, 32], P(('wide', 'act')), may hold values from -0.1875 to 0.1875
- action_head_first: float32 [1024, 32], P(('wide', 'act')), may hold values from -1.9073486e-06 to 1.9073486e-06
- action_head_second: float32 [1024, 32], P(('wide', 'act')), may hold values from 7.0198025e-14 to 2.8619194e-13
Outputs:
- norm_gains_new: float32 [5120], P(('wide', 'act'))
- norm_gains_first_new: float32 [5120], P(('wide', 'act'))
- norm_gains_second_new: float32 [5120], P(('wide', 'act'))
- prefix_kv_new: float32 [2048, 512], P(('wide', 'act'))
- prefix_kv_first_new: float32 [2048, 512], P(('wide', 'act'))
- prefix_kv_second_new: float32 [2048, 512], P(('wide', 'act'))
- action_in_new: float32 [128, 1024], P(('wide', 'act'))
- action_in_first_new: float32 [128, 1024], P(('wide', 'act'))
- action_in_second_new: float32 [128, 1024], P(('wide', 'act'))
- action_qkv_new: float32 [1024, 2560], P(('wide', 'act'))
- action_qkv_first_new: float32 [1024, 2560], P(('wide', 'act'))
- action_qkv_second_new: float32 [1024, 2560], P(('wide', 'act'))
- attn_out_new: float32 [2048, 1024], P(('wide', 'act'))
- attn_out_first_new: float32 [2048, 1024], P(('wide', 'act'))
- attn_out_second_new: float32 [2048, 1024], P(('wide', 'act'))
- action_gate_up_new: float32 [1024, 8192], P(('wide', 'act'))
- action_gate_up_first_new: float32 [1024, 8192], P(('wide', 'act'))
- action_gate_up_second_new: float32 [1024, 8192], P(('wide', 'act'))
- action_down_new: float32 [4096, 1024], P(('wide', 'act'))
- action_down_first_new: float32 [4096, 1024], P(('wide', 'act'))
- action_down_second_new: float32 [4096, 1024], P(('wide', 'act'))
- action_head_new: float32 [1024, 32], P(('wide', 'act'))
- action_head_first_new: float32 [1024, 32], P(('wide', 'act'))
- action_head_second_new: float32 [1024, 32], P(('wide', 'act'))
- loss_sum: float32 [], replicated
- mask_count: float32 [], replicated
- grad_norm: float32 [], replicated
The draws below stay inside these ranges and needn't reach their ends.
Inputs may be any that keep to these rules, and one draw needn't show every extreme that they name: `item_lengths`: each row sums to 10240; its largest entry is exactly 1024.
All inputs are finite; a program needn't handle non-finite values.
Results may differ from the reference program's by a relative error of at most 0.012.
Values may be sent and summed in bfloat16 or wider, within the bound.
No kernel may reach another device: no remote copies, remote signals or barrier semaphores. Data moves between devices by JAX's collectives and lax.ppermute only.
A program may use at most 320 MiB of HBM per device.

```python
import math
import jax
import jax.numpy as jnp
import numpy as np
from jax import lax

D = 2048
DA = 1024
FF = 4096
H = 8
HD = 256
ADIM = 32
TFEAT = 96
S = 50
PMAX = 1024
PAVG = 640
STEP = 10
ITEMS_W = 16
ITEMS = 128
PRE_TOK = 81920
NPARAM = 18519040
N_WIDE = 8


def touch_ends(array, key, least, top_value):
    longest = array.shape.index(max(array.shape))
    spots = []
    for shift in (0, 1):
        where = [jax.random.randint(jax.random.fold_in(key, axis), (), 0, length) for axis, length in enumerate(array.shape)]
        where[longest] = (where[longest] + shift) % array.shape[longest]
        spots.append(tuple(where))
    return array.at[spots[0]].set(least).at[spots[1]].set(top_value)


def shard_levels(rng, shape, cuts, low, high):
    level, own = 1.0, jax.random.fold_in(rng, 6)
    for axis_at, parts in cuts:
        steps = jnp.exp(jax.random.uniform(jax.random.fold_in(own, axis_at), (parts,), jnp.float32, low / len(cuts), high / len(cuts)))
        level = level * jnp.repeat(steps, shape[axis_at] // parts).reshape([-1 if axis == axis_at else 1 for axis in range(len(shape))])
    return level


def profile(count, total, reach, slope):
    portions = [(1 << 20) // math.isqrt(standing ** slope) + 1 for standing in range(2, count + 1)]
    rest, counts = total - reach - (count - 1), [1] * (count - 1)
    while rest > 0:
        movable = [i for i in range(count - 1) if counts[i] < reach]
        mass, left = sum([portions[i] for i in movable]), rest
        for i in movable:
            more = min(reach - counts[i], max(1, left * portions[i] // mass), rest)
            counts[i] = counts[i] + more
            rest = rest - more
    return np.array([reach] + counts)


def uneven_parts(own_key, amount, total, bound, lean):
    if amount == 2:
        one = jax.random.randint(own_key, (), max(1, total - bound), min(bound, total - 1) + 1)
        return jnp.stack([one, total - one])
    sizes = jnp.asarray(profile(amount, total, bound, lean), jnp.int32)
    couples = (amount - 1) // 2
    donor, receiver = sizes[1:1 + 2 * couples:2], sizes[2:2 + 2 * couples:2]
    margin = jnp.minimum(donor - 1, bound - receiver)
    moved = jax.random.randint(jax.random.fold_in(own_key, 1), (couples,), 0, 1 << 20) % (margin + 1)
    sizes = sizes.at[1:1 + 2 * couples:2].set(donor - moved).at[2:2 + 2 * couples:2].set(receiver + moved)
    return sizes[jax.random.permutation(jax.random.fold_in(own_key, 2), amount)]


def normal_values(rng, shape, width, most, split=(), held_as=jnp.bfloat16):
    array = width * jax.random.normal(rng, shape, jnp.float32)
    if split:
        array = array * shard_levels(rng, shape, split, -0.22, 0.18)
    return jnp.clip(array, -most, most).astype(held_as)


def setup_inputs(seed: int = 0) -> dict:
    key_list = jax.random.split(jax.random.key(seed), 31)
    return {
        "prefix_rows": normal_values(key_list[0], (PRE_TOK, D), 1.0, 6.0, ((0, 32),)),
        "item_lengths": jax.vmap(lambda own: uneven_parts(own, ITEMS_W, ITEMS_W * PAVG, PMAX, 1))(jax.random.split(key_list[1], (ITEMS // ITEMS_W))).reshape((ITEMS // ITEMS_W, ITEMS_W)).astype(jnp.int32),
        "action_stretch": normal_values(key_list[2], (ITEMS, S, ADIM), 1.0, 6.0, ((0, 32),), jnp.float32),
        "flow_noise": normal_values(key_list[3], (ITEMS, S, ADIM), 1.0, 6.0, ((0, 32),), jnp.float32),
        "flow_times": jnp.clip(0.05 + 0.95 * jax.random.uniform(key_list[4], (ITEMS,), jnp.float32) ** shard_levels(key_list[4], (ITEMS,), ((0, 32),), -0.2, 0.2), 0.05, 1.0),
        "action_dims": touch_ends(jax.random.randint(key_list[5], (ITEMS,), 7, 19), jax.random.fold_in(key_list[5], 1), 7, 18).astype(jnp.int32),
        "norm_gains": jnp.clip(1.0 + 0.1 * jax.random.normal(key_list[6], (D + 3 * DA,), jnp.float32), 0.5, 1.5),
        "norm_gains_first": normal_values(key_list[7], (D + 3 * DA,), (0.0055 * NPARAM ** -0.5), 1.9073486328125e-05, ((0, 32),), jnp.float32),
        "norm_gains_second": jnp.clip(jnp.exp(math.log(2.861919382035616e-11) - 1.4053426 * jax.random.uniform(key_list[8], (D + 3 * DA,), jnp.float32) ** shard_levels(key_list[8], (D + 3 * DA,), ((0, 32),), -0.2, 0.2)), 7.019802274188525e-12, 2.861919382035616e-11),
        "prefix_kv": normal_values(key_list[9], (D, 2 * HD), D ** -0.5, 0.125, ((0, 32),), jnp.float32),
        "prefix_kv_first": normal_values(key_list[10], (D, 2 * HD), (0.00055 * NPARAM ** -0.5), 1.9073486328125e-06, ((0, 32),), jnp.float32),
        "prefix_kv_second": jnp.clip(jnp.exp(math.log(2.861919414561681e-13) - 1.40534253 * jax.random.uniform(key_list[11], (D, 2 * HD), jnp.float32) ** shard_levels(key_list[11], (D, 2 * HD), ((0, 32),), -0.2, 0.2)), 7.019802491028959e-14, 2.861919414561681e-13),
        "action_in": normal_values(key_list[12], (ADIM + TFEAT, DA), (ADIM + TFEAT) ** -0.5, 0.5, ((0, 32),), jnp.float32),
        "action_in_first": normal_values(key_list[13], (ADIM + TFEAT, DA), (0.00055 * NPARAM ** -0.5), 1.9073486328125e-06, ((0, 32),), jnp.float32),
        "action_in_second": jnp.clip(jnp.exp(math.log(2.861919414561681e-13) - 1.40534253 * jax.random.uniform(key_list[14], (ADIM + TFEAT, DA), jnp.float32) ** shard_levels(key_list[14], (ADIM + TFEAT, DA), ((0, 32),), -0.2, 0.2)), 7.019802491028959e-14, 2.861919414561681e-13),
        "action_qkv": normal_values(key_list[15], (DA, H * HD + 2 * HD), DA ** -0.5, 0.1875, ((0, 32),), jnp.float32),
        "action_qkv_first": normal_values(key_list[16], (DA, H * HD + 2 * HD), (0.00055 * NPARAM ** -0.5), 1.9073486328125e-06, ((0, 32),), jnp.float32),
        "action_qkv_second": jnp.clip(jnp.exp(math.log(2.861919414561681e-13) - 1.40534253 * jax.random.uniform(key_list[17], (DA, H * HD + 2 * HD), jnp.float32) ** shard_levels(key_list[17], (DA, H * HD + 2 * HD), ((0, 32),), -0.2, 0.2)), 7.019802491028959e-14, 2.861919414561681e-13),
        "attn_out": normal_values(key_list[18], (H * HD, DA), (H * HD // 16) ** -0.5, 0.5, ((0, 32),), jnp.float32),
        "attn_out_first": normal_values(key_list[19], (H * HD, DA), (0.00055 * NPARAM ** -0.5), 1.9073486328125e-06, ((0, 32),), jnp.float32),
        "attn_out_second": jnp.clip(jnp.exp(math.log(2.861919414561681e-13) - 1.40534253 * jax.random.uniform(key_list[20], (H * HD, DA), jnp.float32) ** shard_levels(key_list[20], (H * HD, DA), ((0, 32),), -0.2, 0.2)), 7.019802491028959e-14, 2.861919414561681e-13),
        "action_gate_up": normal_values(key_list[21], (DA, 2 * FF), DA ** -0.5, 0.1875, ((0, 32),), jnp.float32),
        "action_gate_up_first": normal_values(key_list[22], (DA, 2 * FF), (0.00055 * NPARAM ** -0.5), 1.9073486328125e-06, ((0, 32),), jnp.float32),
        "action_gate_up_second": jnp.clip(jnp.exp(math.log(2.861919414561681e-13) - 1.40534253 * jax.random.uniform(key_list[23], (DA, 2 * FF), jnp.float32) ** shard_levels(key_list[23], (DA, 2 * FF), ((0, 32),), -0.2, 0.2)), 7.019802491028959e-14, 2.861919414561681e-13),
        "action_down": normal_values(key_list[24], (FF, DA), FF ** -0.5, 0.09375, ((0, 32),), jnp.float32),
        "action_down_first": normal_values(key_list[25], (FF, DA), (0.00055 * NPARAM ** -0.5), 1.9073486328125e-06, ((0, 32),), jnp.float32),
        "action_down_second": jnp.clip(jnp.exp(math.log(2.861919414561681e-13) - 1.40534253 * jax.random.uniform(key_list[26], (FF, DA), jnp.float32) ** shard_levels(key_list[26], (FF, DA), ((0, 32),), -0.2, 0.2)), 7.019802491028959e-14, 2.861919414561681e-13),
        "action_head": normal_values(key_list[27], (DA, ADIM), DA ** -0.5, 0.1875, ((0, 32),), jnp.float32),
        "action_head_first": normal_values(key_list[28], (DA, ADIM), (0.00055 * NPARAM ** -0.5), 1.9073486328125e-06, ((0, 32),), jnp.float32),
        "action_head_second": jnp.clip(jnp.exp(math.log(2.861919414561681e-13) - 1.40534253 * jax.random.uniform(key_list[29], (DA, ADIM), jnp.float32) ** shard_levels(key_list[29], (DA, ADIM), ((0, 32),), -0.2, 0.2)), 7.019802491028959e-14, 2.861919414561681e-13),
    }


HIGHEST = lax.Precision.HIGHEST
NORM_EPS = 1e-06
CLIP_AT = 0.005
BETA_ONE = 0.9
BETA_TWO = 0.95
ADAM_EPS = 1e-08
MATRIX_RATE = 0.02
GAIN_RATE = 0.7
WEIGHT_DECAY = 0.01

@jax.custom_vjp
def low(v):
    return lax.optimization_barrier(v.astype(jnp.bfloat16)).astype(jnp.float32)

@jax.custom_vjp
def low_back(v):
    return v

def low_keep(v):
    return (low(v), None)

def low_pass(kept, grad):
    return (grad,)

def back_keep(v):
    return (v, None)

def back_low(kept, grad):
    return (low(grad),)
low.defvjp(low_keep, low_pass)
low_back.defvjp(back_keep, back_low)

def matmul(matrix_a, matrix_b):
    return jnp.dot(matrix_a, matrix_b, precision=HIGHEST, preferred_element_type=jnp.float32)

def rms_norm(values, scaling):
    return values * lax.rsqrt(lax.optimization_barrier(jnp.mean(values * values, axis=-1, keepdims=True)) + NORM_EPS) * scaling

def time_features(stamps, feat_width):
    half_width = feat_width // 2
    ladder = jnp.arange(half_width, dtype=jnp.float32) / (half_width - 1)
    frequency = 6.283185307179586 / (0.004 * 1000.0 ** ladder)
    angles = stamps[:, None] * frequency[None, :]
    return jnp.concatenate([jnp.sin(angles), jnp.cos(angles)], axis=1)

def glu_unit(gate_in, up_in):
    return jax.nn.gelu(gate_in, approximate=True) * up_in

def adamw(master_w, moment_one, moment_two, gradient, step_rate, decay_rate):
    first_new = BETA_ONE * moment_one + (1.0 - BETA_ONE) * gradient
    second_new = BETA_TWO * moment_two + (1.0 - BETA_TWO) * gradient * gradient
    first_hat = first_new / (1.0 - BETA_ONE ** STEP)
    second_hat = second_new / (1.0 - BETA_TWO ** STEP)
    master_new = master_w - step_rate * (first_hat / (jnp.sqrt(second_hat) + ADAM_EPS) + decay_rate * master_w)
    return (master_new, first_new, second_new)

def group_loss(weight_set, prefix, lengths, actions, noise_in, stamps, item_dims):
    gains_all, kv_proj, in_proj, qkv_proj, out_att, gate_up, down_proj, out_proj = weight_set
    model_width = prefix.shape[1]
    inner_width = out_proj.shape[0]
    query_width = out_att.shape[0]
    head_size = (qkv_proj.shape[1] - query_width) // 2
    head_count = query_width // head_size
    hidden_width = down_proj.shape[0]
    item_count, step_count, action_width = actions.shape
    gain_pre = gains_all[:model_width]
    gain_one = gains_all[model_width:model_width + inner_width]
    gain_two = gains_all[model_width + inner_width:model_width + 2 * inner_width]
    gain_three = gains_all[model_width + 2 * inner_width:]
    prefix_keys = low_back(low(matmul(low(rms_norm(prefix, gain_pre)), kv_proj)))
    ends_at = jnp.cumsum(lengths).astype(jnp.int32)
    starts = ends_at - lengths
    window_first = jnp.minimum(starts, prefix_keys.shape[0] - PMAX)
    places = window_first[:, None] + jnp.arange(PMAX, dtype=jnp.int32)[None, :]
    live_keys = (places >= starts[:, None]) & (places < ends_at[:, None])
    window = prefix_keys[places]
    blend_t = stamps[:, None, None]
    noisy_acts = blend_t * noise_in + (1.0 - blend_t) * actions
    stamp_feats = jnp.broadcast_to(time_features(stamps, TFEAT)[:, None, :], (item_count, step_count, TFEAT))
    features = low(jnp.concatenate([noisy_acts, stamp_feats], axis=2).reshape(item_count * step_count, -1))
    base_res = low_back(matmul(features, in_proj))
    attn_in = low(rms_norm(base_res, gain_one))
    projected = matmul(attn_in, qkv_proj)
    queries = low_back(low(projected[:, :query_width])).reshape(item_count, step_count, head_count, head_size)
    own_kv = low_back(low(projected[:, query_width:])).reshape(item_count, step_count, 2 * head_size)
    all_kv = jnp.concatenate([window, own_kv], axis=1)
    key_part = all_kv[:, :, :head_size]
    value_part = all_kv[:, :, head_size:]
    key_live = jnp.concatenate([live_keys, jnp.ones((item_count, step_count), jnp.bool_)], axis=1)
    scores = low_back(jnp.einsum('ishd,ikd->ihsk', queries, key_part, precision=HIGHEST) * head_size ** (-0.5))
    scores = jnp.where(key_live[:, None, None, :], scores, -1e+30)
    shifted = jnp.exp(scores - lax.optimization_barrier(jnp.max(scores, axis=-1, keepdims=True)))
    attn_probs = shifted / lax.optimization_barrier(jnp.sum(shifted, axis=-1, keepdims=True))
    attended = jnp.einsum('ihsk,ikd->ishd', low(attn_probs), value_part, precision=HIGHEST)
    attended = low_back(low(attended.reshape(item_count * step_count, query_width)))
    mid_res = base_res + low_back(matmul(attended, out_att))
    mlp_in = low(rms_norm(mid_res, gain_two))
    gate_vals = low_back(matmul(mlp_in, gate_up))
    hidden = low(glu_unit(gate_vals[:, :hidden_width], gate_vals[:, hidden_width:]))
    top_res = mid_res + low_back(matmul(hidden, down_proj))
    head_in = low(rms_norm(top_res, gain_three))
    predicted = low_back(matmul(head_in, out_proj)).reshape(item_count, step_count, action_width)
    keep_dims = jnp.arange(action_width)[None, :] < item_dims[:, None]
    mismatch = predicted - (noise_in - actions)
    return jnp.sum(jnp.where(keep_dims[:, None, :], mismatch * mismatch, 0.0))

def reference(prefix_rows, item_lengths, action_stretch, flow_noise, flow_times, action_dims, norm_gains, norm_gains_first, norm_gains_second, prefix_kv, prefix_kv_first, prefix_kv_second, action_in, action_in_first, action_in_second, action_qkv, action_qkv_first, action_qkv_second, attn_out, attn_out_first, attn_out_second, action_gate_up, action_gate_up_first, action_gate_up_second, action_down, action_down_first, action_down_second, action_head, action_head_first, action_head_second):
    masters = (norm_gains, prefix_kv, action_in, action_qkv, attn_out, action_gate_up, action_down, action_head)
    moments_one = (norm_gains_first, prefix_kv_first, action_in_first, action_qkv_first, attn_out_first, action_gate_up_first, action_down_first, action_head_first)
    moments_two = (norm_gains_second, prefix_kv_second, action_in_second, action_qkv_second, attn_out_second, action_gate_up_second, action_down_second, action_head_second)
    group_count = N_WIDE
    prefix_all = prefix_rows.astype(jnp.float32).reshape(group_count, -1, prefix_rows.shape[1])
    stretches = action_stretch.reshape(group_count, -1, action_stretch.shape[1], action_stretch.shape[2])
    noises = flow_noise.reshape(stretches.shape)
    stamps = flow_times.reshape(group_count, -1)
    dim_groups = action_dims.reshape(group_count, -1)
    mask_count = (action_stretch.shape[1] * jnp.sum(action_dims)).astype(jnp.float32)

    def total_loss(weight_set):
        rounded = tuple((low(master_w) for master_w in weight_set))

        def one_group(pieces):
            return group_loss(rounded, *pieces)
        group_sums = lax.map(jax.checkpoint(one_group), (prefix_all, item_lengths, stretches, noises, stamps, dim_groups))
        return jnp.sum(group_sums)
    loss_sum, pullback = jax.vjp(total_loss, masters)
    gradients, = pullback(jnp.ones((), jnp.float32) / mask_count)
    squares = sum((jnp.sum(grad_one * grad_one) for grad_one in gradients))
    grad_norm = jnp.sqrt(squares)
    clip_factor = jnp.minimum(1.0, CLIP_AT / (grad_norm + 1e-06))
    step_rates = (GAIN_RATE,) + (MATRIX_RATE,) * 7
    decay_rates = (0.0,) + (WEIGHT_DECAY,) * 7
    updated = []
    for master_w, moment_one, moment_two, gradient, step_rate, decay_rate in zip(masters, moments_one, moments_two, gradients, step_rates, decay_rates):
        updated.extend(adamw(master_w, moment_one, moment_two, gradient * clip_factor, step_rate, decay_rate))
    return (updated[0], updated[1], updated[2], updated[3], updated[4], updated[5], updated[6], updated[7], updated[8], updated[9], updated[10], updated[11], updated[12], updated[13], updated[14], updated[15], updated[16], updated[17], updated[18], updated[19], updated[20], updated[21], updated[22], updated[23], loss_sum, mask_count, grad_norm)
```

```python
import jax
import jax.numpy as jnp
from jax import lax
from jax.sharding import PartitionSpec as P

TFEAT = 96
PMAX = 1024
STEP = 10


NORM_EPS = 1e-06
CLIP_AT = 0.005
BETA_ONE = 0.9
BETA_TWO = 0.95
ADAM_EPS = 1e-08
MATRIX_RATE = 0.02
GAIN_RATE = 0.7
WEIGHT_DECAY = 0.01


def product(matrix_a, matrix_b):
    return jnp.dot(matrix_a, matrix_b, preferred_element_type=jnp.float32)


def norm_forward(values, scaling):
    inverse = lax.rsqrt(jnp.mean(values * values, axis=-1, keepdims=True) + NORM_EPS)
    unit_vals = values * inverse
    return (unit_vals * scaling, unit_vals, inverse)


def norm_backward(grad_out, unit_vals, inverse, scaling):
    grad_unit = grad_out * scaling
    grad_in = inverse * (
        grad_unit - unit_vals * jnp.mean(grad_unit * unit_vals, axis=-1, keepdims=True)
    )
    return (grad_in, jnp.sum(grad_out * unit_vals, axis=0))


def time_features(stamps, feat_width):
    half_width = feat_width // 2
    ladder = jnp.arange(half_width, dtype=jnp.float32) / (half_width - 1)
    frequency = 6.283185307179586 / (0.004 * 1000.0**ladder)
    angles = stamps[:, None] * frequency[None, :]
    return jnp.concatenate([jnp.sin(angles), jnp.cos(angles)], axis=1)


def glu_unit(gate_in, up_in):
    return jax.nn.gelu(gate_in, approximate=True) * up_in


def adamw(master_w, moment_one, moment_two, gradient, step_rate, decay_rate):
    first_new = BETA_ONE * moment_one + (1.0 - BETA_ONE) * gradient
    second_new = BETA_TWO * moment_two + (1.0 - BETA_TWO) * gradient * gradient
    first_hat = first_new / (1.0 - BETA_ONE**STEP)
    second_hat = second_new / (1.0 - BETA_TWO**STEP)
    master_new = master_w - step_rate * (
        first_hat / (jnp.sqrt(second_hat) + ADAM_EPS) + decay_rate * master_w
    )
    return (master_new, first_new, second_new)


def split_gains(gains_all, model_width, inner_width):
    gains_f = gains_all.astype(jnp.float32)
    return (
        gains_f[:model_width],
        gains_f[model_width : model_width + inner_width],
        gains_f[model_width + inner_width : model_width + 2 * inner_width],
        gains_f[model_width + 2 * inner_width :],
    )


def flip(block, axis, bit):
    size = lax.axis_size(axis)
    return lax.ppermute(block, axis, [(place, place ^ bit) for place in range(size)])


def place_bits():
    bits = []
    for axis in ("wide", "act"):
        bit = lax.axis_size(axis) // 2
        while bit:
            bits.append((axis, bit))
            bit //= 2
    return bits


def my_bit(axis, bit):
    return (lax.axis_index(axis) // bit) % 2


CORE = ("act", 1)


def routes():
    bits = place_bits()
    act_bits = [b for b in bits if b[0] == "act" and b[1] > 1]
    wide_far = [b for b in bits if b[0] == "wide" and b[1] > 1]
    wide_near = [b for b in bits if b == ("wide", 1)]
    return (
        act_bits + wide_far + wide_near,
        wide_near + wide_far + act_bits,
        wide_far + act_bits + wide_near,
        wide_far + wide_near + act_bits,
    )


def collect(shard, route):
    bits = place_bits()
    held = []
    block = shard
    for bit in route:
        other = flip(block, *bit)
        low_side = my_bit(*bit) == 0
        first = jnp.where(low_side, block, other)
        second = jnp.where(low_side, other, block)
        held.append(bit)
        held.sort(key=bits.index)
        block = jnp.stack([first, second], axis=held.index(bit))
    return block


def disperse(block, route):
    bits = place_bits()
    held = sorted(route, key=bits.index)
    for number, bit in enumerate(reversed(route)):
        at = held.index(bit)
        mine = my_bit(*bit)
        send = lax.dynamic_index_in_dim(block, 1 - mine, at, keepdims=False)
        keep = lax.dynamic_index_in_dim(block, mine, at, keepdims=False)
        other = flip(send, *bit)
        block = keep.astype(jnp.float32) + other.astype(jnp.float32)
        if number < len(route) - 1:
            block = block.astype(jnp.bfloat16)
        held.remove(bit)
    return block


def total(value):
    for bit in reversed(place_bits()):
        value = value + flip(value, *bit)
    return value


def pack_rows(parts, width):
    lead = parts[0].shape[0]
    rows = []
    for part in parts:
        flat = part.reshape(lead, -1)
        short = -flat.shape[1] % width
        rows.append(jnp.pad(flat, ((0, 0), (0, short))).reshape(lead, -1, width))
    packed = jnp.concatenate(rows, axis=1)
    return jnp.pad(packed, ((0, 0), (0, -packed.shape[1] % 16), (0, 0)))


def unpack_rows(packed, shapes):
    lead, width = packed.shape[0], packed.shape[2]
    parts, at = [], 0
    for shape in shapes:
        size = 1
        for extent in shape:
            size *= extent
        count = -(-size // width)
        flat = packed[:, at : at + count].reshape(lead, -1)[:, :size]
        parts.append(flat.reshape((lead,) + tuple(shape)))
        at += count
    return parts


def core_half(block, core):
    return lax.dynamic_index_in_dim(block, core, 2, keepdims=False)


def on_device(
    prefix_rows,
    item_lengths,
    action_stretch,
    flow_noise,
    flow_times,
    action_dims,
    norm_gains,
    norm_gains_first,
    norm_gains_second,
    prefix_kv,
    prefix_kv_first,
    prefix_kv_second,
    action_in,
    action_in_first,
    action_in_second,
    action_qkv,
    action_qkv_first,
    action_qkv_second,
    attn_out,
    attn_out_first,
    attn_out_second,
    action_gate_up,
    action_gate_up_first,
    action_gate_up_second,
    action_down,
    action_down_first,
    action_down_second,
    action_head,
    action_head_first,
    action_head_second,
):
    masters = (
        norm_gains,
        prefix_kv,
        action_in,
        action_qkv,
        attn_out,
        action_gate_up,
        action_down,
        action_head,
    )
    moments_one = (
        norm_gains_first,
        prefix_kv_first,
        action_in_first,
        action_qkv_first,
        attn_out_first,
        action_gate_up_first,
        action_down_first,
        action_head_first,
    )
    moments_two = (
        norm_gains_second,
        prefix_kv_second,
        action_in_second,
        action_qkv_second,
        attn_out_second,
        action_gate_up_second,
        action_down_second,
        action_head_second,
    )
    inner_width = action_down.shape[1]
    device_count = lax.axis_size("wide") * lax.axis_size("act")
    half_count = device_count // 2
    core = lax.axis_index("act") % 2
    route_one, route_two, route_three, route_four = routes()
    every_bit = place_bits()
    lanes = [bit for bit in every_bit if bit != CORE]
    low_precision = jnp.bfloat16

    small_shards = (prefix_kv, action_in, action_head, norm_gains)
    pack_width = prefix_kv.shape[1]
    small = pack_rows([part.astype(low_precision)[None] for part in small_shards], pack_width)[0]
    small = collect(small, route_three + [CORE])
    small_all = unpack_rows(
        small.reshape((device_count,) + small.shape[-2:]), [part.shape for part in small_shards]
    )
    kv_proj, in_proj, out_proj, gains_all = (
        part.reshape((-1,) + part.shape[2:]) for part in small_all
    )
    qkv_proj = collect(action_qkv.astype(low_precision), route_four + [CORE])
    qkv_proj = qkv_proj.reshape(-1, action_qkv.shape[1])
    out_att = collect(attn_out.astype(low_precision), route_three + [CORE])
    out_att = out_att.reshape(-1, inner_width)
    hidden_width = action_gate_up.shape[1] // 2
    unit_block = action_down.shape[0]
    gate_rows = action_gate_up.shape[0]
    sides = action_gate_up.astype(low_precision).reshape(gate_rows, 2 * half_count, 2, unit_block)
    sides_kept = core_half(sides, core).reshape(gate_rows, hidden_width)
    sides_sent = core_half(sides, 1 - core).reshape(gate_rows, hidden_width)
    sides_other = flip(sides_sent, *CORE)
    sides = jnp.concatenate(
        [jnp.where(core == 0, sides_kept, sides_other), jnp.where(core == 0, sides_other, sides_kept)]
    )
    half_hidden = hidden_width // 2
    gate_proj = collect(sides[:, :half_hidden], route_one).reshape(inner_width, half_hidden)
    up_proj = collect(sides[:, half_hidden:], route_two).reshape(inner_width, half_hidden)
    down_low = action_down.astype(low_precision)
    half_inner = inner_width // 2
    down_one = collect(down_low[:, :half_inner], route_three).reshape(half_hidden, half_inner)
    down_two = collect(down_low[:, half_inner:], route_two).reshape(half_hidden, half_inner)
    down_proj = jnp.concatenate([down_one, down_two], axis=1)

    counted = total(
        jnp.float32(action_stretch.shape[1]) * jnp.sum(action_dims).astype(jnp.float32)
    )

    model_width = prefix_rows.shape[1]
    query_width = out_att.shape[0]
    head_size = (qkv_proj.shape[1] - query_width) // 2
    head_count = query_width // head_size
    item_count, step_count, action_width = action_stretch.shape
    row_count = item_count * step_count
    gain_pre, gain_one, gain_two, gain_three = split_gains(gains_all, model_width, inner_width)
    pre_normed, pre_unit, pre_inverse = norm_forward(prefix_rows.astype(jnp.float32), gain_pre)
    pre_in = pre_normed.astype(low_precision)
    pre_keys = product(pre_in, kv_proj).astype(low_precision)
    act_lanes = [bit for bit in lanes if bit[0] == "act"]
    stream = collect(pre_keys, act_lanes + [CORE]).reshape(-1, pre_keys.shape[1])
    stream_len = stream.shape[0]
    lengths = item_lengths[0]
    ends_at = jnp.cumsum(lengths)
    starts = ends_at - lengths
    offset = lax.axis_index("act") * item_count
    mine_start = lax.dynamic_slice_in_dim(starts, offset, item_count)
    mine_end = lax.dynamic_slice_in_dim(ends_at, offset, item_count)
    window_first = jnp.minimum(mine_start, stream_len - PMAX)
    places = window_first[:, None] + jnp.arange(PMAX, dtype=jnp.int32)[None, :]
    live_keys = (places >= mine_start[:, None]) & (places < mine_end[:, None])
    window = stream[places]
    blend_t = flow_times[:, None, None]
    noisy_acts = blend_t * flow_noise + (1.0 - blend_t) * action_stretch
    stamp_feats = jnp.broadcast_to(
        time_features(flow_times, TFEAT)[:, None, :], (item_count, step_count, TFEAT)
    )
    features = (
        jnp.concatenate([noisy_acts, stamp_feats], axis=2)
        .reshape(row_count, -1)
        .astype(low_precision)
    )
    base_res = product(features, in_proj)
    attn_normed, unit_one, inverse_one = norm_forward(base_res, gain_one)
    attn_in = attn_normed.astype(low_precision)
    projected = product(attn_in, qkv_proj)
    queries = (
        projected[:, :query_width]
        .astype(low_precision)
        .reshape(item_count, step_count, head_count, head_size)
    )
    own_kv = (
        projected[:, query_width:]
        .astype(low_precision)
        .reshape(item_count, step_count, 2 * head_size)
    )
    all_kv = jnp.concatenate([window, own_kv], axis=1)
    key_part = all_kv[:, :, :head_size]
    value_part = all_kv[:, :, head_size:]
    key_live = jnp.concatenate([live_keys, jnp.ones((item_count, step_count), jnp.bool_)], axis=1)
    scale = head_size ** (-0.5)
    scores = (
        jnp.einsum("ishd,ikd->ihsk", queries, key_part, preferred_element_type=jnp.float32) * scale
    )
    scores = jnp.where(key_live[:, None, None, :], scores, -1e30)
    shifted = jnp.exp(scores - jnp.max(scores, axis=-1, keepdims=True))
    attn_probs = shifted / jnp.sum(shifted, axis=-1, keepdims=True)
    attended = jnp.einsum(
        "ihsk,ikd->ishd",
        attn_probs.astype(low_precision),
        value_part,
        preferred_element_type=jnp.float32,
    )
    attended = attended.reshape(row_count, query_width).astype(low_precision)
    mid_res = base_res + product(attended, out_att)
    mlp_normed, unit_two, inverse_two = norm_forward(mid_res, gain_two)
    mlp_in = mlp_normed.astype(low_precision)
    mlp_pair = jnp.concatenate([mlp_in, flip(mlp_in, *CORE)])
    gate_part = product(mlp_pair, gate_proj)
    up_part = product(mlp_pair, up_proj)
    hidden = glu_unit(gate_part, up_part).astype(low_precision)
    down_pair = product(hidden, down_proj)
    top_res = mid_res + down_pair[:row_count] + flip(down_pair[row_count:], *CORE)
    head_normed, unit_three, inverse_three = norm_forward(top_res, gain_three)
    head_in = head_normed.astype(low_precision)
    predicted = product(head_in, out_proj).reshape(item_count, step_count, action_width)
    keep_dims = (jnp.arange(action_width)[None, :] < action_dims[:, None]).astype(jnp.float32)
    mismatch = (predicted - (flow_noise - action_stretch)) * keep_dims[:, None, :]
    loss_sum = total(jnp.sum(mismatch * mismatch))

    grad_pred = (2.0 * mismatch / counted).reshape(row_count, -1).astype(low_precision)
    grad_head = product(head_in.T, grad_pred)
    grad_top, gain_grad_three = norm_backward(
        product(grad_pred, out_proj.T), unit_three, inverse_three, gain_three
    )
    grad_mlp = grad_top.astype(low_precision)
    grad_mlp_pair = jnp.concatenate([grad_mlp, flip(grad_mlp, *CORE)])
    grad_down = product(hidden.T, grad_mlp_pair).astype(low_precision)
    lane_shape = (2,) * len(lanes)
    down_shape = lane_shape + (unit_block, half_inner)
    grad_down = jnp.concatenate(
        [
            disperse(grad_down[:, :half_inner].reshape(down_shape), route_three),
            disperse(grad_down[:, half_inner:].reshape(down_shape), route_two),
        ],
        axis=1,
    )
    grad_hidden = product(grad_mlp_pair, down_proj.T)
    glu_value, glu_pull = jax.vjp(glu_unit, gate_part, up_part)
    grad_gate, grad_up = glu_pull(grad_hidden)
    grad_gate = grad_gate.astype(low_precision)
    grad_up = grad_up.astype(low_precision)
    side_shape = lane_shape + (2 * gate_rows, half_hidden)
    grad_gate_w = product(mlp_pair.T, grad_gate).astype(low_precision).reshape(side_shape)
    grad_up_w = product(mlp_pair.T, grad_up).astype(low_precision).reshape(side_shape)
    grad_sides = jnp.concatenate(
        [disperse(grad_gate_w, route_one), disperse(grad_up_w, route_two)], axis=1
    ).astype(low_precision)
    grad_sides = grad_sides.reshape(2, gate_rows, hidden_width)
    sides_kept = lax.dynamic_index_in_dim(grad_sides, core, 0, keepdims=False)
    sides_sent = lax.dynamic_index_in_dim(grad_sides, 1 - core, 0, keepdims=False)
    sides_other = flip(sides_sent, *CORE)
    sides_kept = sides_kept.reshape(gate_rows, 2 * half_count, 1, unit_block)
    sides_other = sides_other.reshape(gate_rows, 2 * half_count, 1, unit_block)
    grad_gate_up = jnp.concatenate(
        [jnp.where(core == 0, sides_kept, sides_other), jnp.where(core == 0, sides_other, sides_kept)],
        axis=2,
    ).reshape(action_gate_up.shape)
    grad_mlp_in = product(grad_gate, gate_proj.T) + product(grad_up, up_proj.T)
    grad_mlp_in = grad_mlp_in[:row_count] + flip(grad_mlp_in[row_count:], *CORE)
    grad_mlp_in, gain_grad_two = norm_backward(grad_mlp_in, unit_two, inverse_two, gain_two)
    grad_mid = grad_top + grad_mlp_in
    grad_branch = grad_mid.astype(low_precision)
    grad_out_att = product(attended.T, grad_branch).astype(low_precision)
    every_shape = (2,) * len(every_bit)
    grad_out_att = disperse(
        grad_out_att.reshape(every_shape + attn_out.shape), route_three + [CORE]
    )
    grad_attended = product(grad_branch, out_att.T).astype(low_precision).reshape(queries.shape)
    grad_probs = jnp.einsum(
        "ishd,ikd->ihsk", grad_attended, value_part, preferred_element_type=jnp.float32
    )
    grad_values = jnp.einsum(
        "ihsk,ishd->ikd",
        attn_probs.astype(low_precision),
        grad_attended,
        preferred_element_type=jnp.float32,
    )
    grad_scores = attn_probs * (
        grad_probs - jnp.sum(grad_probs * attn_probs, axis=-1, keepdims=True)
    )
    grad_scores = grad_scores.astype(low_precision)
    grad_queries = (
        jnp.einsum("ihsk,ikd->ishd", grad_scores, key_part, preferred_element_type=jnp.float32)
        * scale
    )
    grad_keys = (
        jnp.einsum("ihsk,ishd->ikd", grad_scores, queries, preferred_element_type=jnp.float32)
        * scale
    )
    grad_all_kv = jnp.concatenate([grad_keys, grad_values], axis=2)
    grad_own = grad_all_kv[:, PMAX:].reshape(row_count, 2 * head_size)
    grad_projected = jnp.concatenate(
        [grad_queries.reshape(row_count, query_width), grad_own], axis=1
    ).astype(low_precision)
    grad_qkv = product(attn_in.T, grad_projected).astype(low_precision)
    grad_qkv = disperse(grad_qkv.reshape(every_shape + action_qkv.shape), route_four + [CORE])
    grad_attn_in, gain_grad_one = norm_backward(
        product(grad_projected, qkv_proj.T), unit_one, inverse_one, gain_one
    )
    grad_base = (grad_mid + grad_attn_in).astype(low_precision)
    grad_in = product(features.T, grad_base)
    spread = (
        jnp.zeros((stream_len, 2 * head_size), low_precision)
        .at[places.reshape(-1)]
        .add(grad_all_kv[:, :PMAX].reshape(-1, 2 * head_size).astype(low_precision))
    )
    act_shape = (2,) * (len(act_lanes) + 1)
    grad_prefix = disperse(
        spread.reshape(act_shape + pre_keys.shape), act_lanes + [CORE]
    ).astype(low_precision)
    grad_kv = product(pre_in.T, grad_prefix)
    gain_grad_pre = jnp.sum(grad_kv * kv_proj.astype(jnp.float32), axis=1) / gain_pre
    grad_gains = jnp.concatenate([gain_grad_pre, gain_grad_one, gain_grad_two, gain_grad_three])
    small_grads = [
        part.astype(low_precision).reshape((device_count,) + shard.shape)
        for part, shard in zip((grad_kv, grad_in, grad_head, grad_gains), small_shards)
    ]
    small_grads = pack_rows(small_grads, pack_width)
    small_grads = disperse(
        small_grads.reshape(every_shape + small_grads.shape[1:]), route_three + [CORE]
    )
    small_grads = unpack_rows(small_grads[None], [part.shape for part in small_shards])
    grad_kv, grad_in, grad_head, grad_gains = (part[0] for part in small_grads)
    gradients = (
        grad_gains,
        grad_kv,
        grad_in,
        grad_qkv,
        grad_out_att,
        grad_gate_up.astype(jnp.float32),
        grad_down,
        grad_head,
    )
    local_squares = sum((jnp.sum(grad_one * grad_one) for grad_one in gradients))
    grad_norm = jnp.sqrt(total(local_squares))
    clip_factor = jnp.minimum(1.0, CLIP_AT / (grad_norm + 1e-06))
    step_rates = (GAIN_RATE,) + (MATRIX_RATE,) * 7
    decay_rates = (0.0,) + (WEIGHT_DECAY,) * 7
    updated = []
    for master_w, moment_one, moment_two, gradient, step_rate, decay_rate in zip(
        masters, moments_one, moments_two, gradients, step_rates, decay_rates
    ):
        updated.extend(
            adamw(master_w, moment_one, moment_two, gradient * clip_factor, step_rate, decay_rate)
        )
    return (
        updated[0],
        updated[1],
        updated[2],
        updated[3],
        updated[4],
        updated[5],
        updated[6],
        updated[7],
        updated[8],
        updated[9],
        updated[10],
        updated[11],
        updated[12],
        updated[13],
        updated[14],
        updated[15],
        updated[16],
        updated[17],
        updated[18],
        updated[19],
        updated[20],
        updated[21],
        updated[22],
        updated[23],
        loss_sum,
        counted,
        grad_norm,
    )


def solution(mesh):
    placed = (
        P(("wide", "act"), None),
        P("wide", None),
        P(("wide", "act"), None, None),
        P(("wide", "act"), None, None),
        P(("wide", "act")),
        P(("wide", "act")),
        P(("wide", "act")),
        P(("wide", "act")),
        P(("wide", "act")),
        P(("wide", "act"), None),
        P(("wide", "act"), None),
        P(("wide", "act"), None),
        P(("wide", "act"), None),
        P(("wide", "act"), None),
        P(("wide", "act"), None),
        P(("wide", "act"), None),
        P(("wide", "act"), None),
        P(("wide", "act"), None),
        P(("wide", "act"), None),
        P(("wide", "act"), None),
        P(("wide", "act"), None),
        P(("wide", "act"), None),
        P(("wide", "act"), None),
        P(("wide", "act"), None),
        P(("wide", "act"), None),
        P(("wide", "act"), None),
        P(("wide", "act"), None),
        P(("wide", "act"), None),
        P(("wide", "act"), None),
        P(("wide", "act"), None),
    )
    return jax.shard_map(
        on_device,
        mesh=mesh,
        in_specs=placed,
        out_specs=(
            P(("wide", "act")),
            P(("wide", "act")),
            P(("wide", "act")),
            P(("wide", "act"), None),
            P(("wide", "act"), None),
            P(("wide", "act"), None),
            P(("wide", "act"), None),
            P(("wide", "act"), None),
            P(("wide", "act"), None),
            P(("wide", "act"), None),
            P(("wide", "act"), None),
            P(("wide", "act"), None),
            P(("wide", "act"), None),
            P(("wide", "act"), None),
            P(("wide", "act"), None),
            P(("wide", "act"), None),
            P(("wide", "act"), None),
            P(("wide", "act"), None),
            P(("wide", "act"), None),
            P(("wide", "act"), None),
            P(("wide", "act"), None),
            P(("wide", "act"), None),
            P(("wide", "act"), None),
            P(("wide", "act"), None),
            P(),
            P(),
            P(),
        ),
        check_vma=False,
    )
```

```python
import functools

import jax
import jax.numpy as jnp
from jax import lax
from jax.experimental import pallas as pl
from jax.experimental.pallas import tpu as pltpu
from jax.sharding import Mesh
from jax.sharding import PartitionSpec as P

TFEAT = 96
PMAX = 1024
STEP = 10
KERNEL_BYTES = 48 * 1024 * 1024


NORM_EPS = 1e-06
CLIP_AT = 0.005
BETA_ONE = 0.9
BETA_TWO = 0.95
ADAM_EPS = 1e-08
MATRIX_RATE = 0.02
GAIN_RATE = 0.7
WEIGHT_DECAY = 0.01


def product(matrix_a, matrix_b):
    return jnp.dot(matrix_a, matrix_b, preferred_element_type=jnp.float32)


def norm_forward(values, scaling):
    inverse = lax.rsqrt(jnp.mean(values * values, axis=-1, keepdims=True) + NORM_EPS)
    unit_vals = values * inverse
    return (unit_vals * scaling, unit_vals, inverse)


def norm_backward(grad_out, unit_vals, inverse, scaling):
    grad_unit = grad_out * scaling
    grad_in = inverse * (
        grad_unit - unit_vals * jnp.mean(grad_unit * unit_vals, axis=-1, keepdims=True)
    )
    return (grad_in, jnp.sum(grad_out * unit_vals, axis=0))


def time_features(stamps, feat_width):
    half_width = feat_width // 2
    ladder = jnp.arange(half_width, dtype=jnp.float32) / (half_width - 1)
    frequency = 6.283185307179586 / (0.004 * 1000.0**ladder)
    angles = stamps[:, None] * frequency[None, :]
    return jnp.concatenate([jnp.sin(angles), jnp.cos(angles)], axis=1)


def glu_unit(gate_in, up_in):
    return jax.nn.gelu(gate_in, approximate=True) * up_in


def adamw(master_w, moment_one, moment_two, gradient, step_rate, decay_rate):
    first_new = BETA_ONE * moment_one + (1.0 - BETA_ONE) * gradient
    second_new = BETA_TWO * moment_two + (1.0 - BETA_TWO) * gradient * gradient
    first_hat = first_new / (1.0 - BETA_ONE**STEP)
    second_hat = second_new / (1.0 - BETA_TWO**STEP)
    master_new = master_w - step_rate * (
        first_hat / (jnp.sqrt(second_hat) + ADAM_EPS) + decay_rate * master_w
    )
    return (master_new, first_new, second_new)


def split_gains(gains_all, model_width, inner_width):
    gains_f = gains_all.astype(jnp.float32)
    return (
        gains_f[:model_width],
        gains_f[model_width : model_width + inner_width],
        gains_f[model_width + inner_width : model_width + 2 * inner_width],
        gains_f[model_width + 2 * inner_width :],
    )


AXES = ("wide", "row", "core")
CORE = 1


def device_count():
    return lax.axis_size(AXES)


def act_count():
    return lax.axis_size(("row", "core"))


def flip(block, mask):
    return lax.ppermute(block, AXES, [(place, place ^ mask) for place in range(device_count())])


def my_bit(mask):
    return (lax.axis_index(AXES) // mask) % 2


def bits_between(low, high):
    bits = []
    while low < high:
        bits.append(low)
        low *= 2
    return bits[::-1]


def row_bits():
    return bits_between(2, act_count())


def near_bit():
    return act_count()


def far_bits():
    return bits_between(2 * act_count(), device_count())


def combos(bits):
    masks = [0]
    for bit in bits:
        masks = [mask + more for mask in masks for more in (0, bit)]
    return masks


def settle(blocks, bits):
    for number, bit in enumerate(bits):
        step = len(blocks) >> (number + 1)
        swap = my_bit(bit) == 1
        blocks = [jnp.where(swap, blocks[at ^ step], blocks[at]) for at in range(len(blocks))]
    return blocks


def fetch(block, bits):
    blocks = [block if mask == 0 else flip(block, mask) for mask in combos(bits)]
    return jnp.stack(settle(blocks, bits))


def double(block, bit, at):
    other = flip(block, bit)
    return jnp.stack(settle([block, other], [bit]), axis=at)


def collect_plane(block):
    half = block.shape[2] // 2
    one, two = block[:, :, :half], block[:, :, half:]
    near = double(two, near_bit(), 1)
    for bit in row_bits():
        one = double(one, bit, -3)
    one = one.reshape(one.shape[0], -1, *one.shape[-2:])
    one = double(one, near_bit(), 1)
    for bit in row_bits():
        near = double(near, bit, -3)
    near = near.reshape(one.shape)
    return jnp.concatenate([one, near], axis=-1)


def place_index(bits):
    index = 0
    for bit in bits:
        index = 2 * index + my_bit(bit)
    return index


def pick(block, index, at):
    return lax.dynamic_index_in_dim(block, index, at, keepdims=False)


def wide_sum(blocks):
    return sum(block.astype(jnp.float32) for block in blocks)


def halve(block, bit, at):
    mine = my_bit(bit)
    other = flip(pick(block, 1 - mine, at), bit)
    return wide_sum([pick(block, mine, at), other]).astype(jnp.bfloat16)


def hand_out(block, bits):
    mine = place_index(bits)
    blocks = [pick(block, mine, 0)]
    for number, mask in enumerate(combos(bits)):
        if mask:
            blocks.append(flip(pick(block, mine ^ number, 0), mask))
    return wide_sum(blocks)


def disperse(block):
    rows, columns = block.shape[1:]
    far = 2 ** len(far_bits())
    row_dims = (2,) * len(row_bits())
    block = halve(block.reshape(-1, 2, rows, columns), CORE, 1)
    half = columns // 2
    halves = []
    for part, near_first in ((block[..., :half], False), (block[..., half:], True)):
        part = part.reshape((far, 2) + row_dims + (rows, half))
        if near_first:
            part = halve(part, near_bit(), 1)
        for bit in row_bits():
            part = halve(part, bit, 1 if near_first else 2)
        if not near_first:
            part = halve(part, near_bit(), 1)
        halves.append(hand_out(part, far_bits()))
    return jnp.concatenate(halves, axis=1)


def disperse_small(block):
    rows, columns = block.shape[1:]
    far = 2 ** len(far_bits())
    block = halve(block.reshape(-1, 2, rows, columns), CORE, 1)
    block = block.reshape(far, -1, rows, columns).swapaxes(0, 1)
    block = hand_out(block, [near_bit()] + row_bits()).astype(jnp.bfloat16)
    return hand_out(block, far_bits())


def total(value):
    for bit in bits_between(1, device_count())[::-1]:
        value = value + flip(value, bit)
    return value


def share_rows(block):
    for bit in row_bits() + [CORE]:
        block = jnp.concatenate([block, flip(block, bit)])
    return block


def return_rows(block):
    for bit in [CORE] + row_bits()[::-1]:
        half = block.shape[0] // 2
        other = flip(block[half:].astype(jnp.bfloat16), bit)
        block = block[:half] + other.astype(jnp.float32)
    return block


def swap_in(block):
    rows, groups, size, unit = block.shape
    bits = row_bits() + [CORE]
    block = block.reshape((rows, groups) + (2,) * len(bits) + (unit,))
    for done, bit in enumerate(bits):
        mine = my_bit(bit)
        other = flip(pick(block, 1 - mine, done + 2), bit)
        block = jnp.stack(settle([pick(block, mine, done + 2), other], [bit]), axis=done)
    return block.reshape(size * rows, groups * unit)


def swap_out(block, groups):
    bits = row_bits() + [CORE]
    size = act_count()
    rows, unit = block.shape[0] // size, block.shape[1] // groups
    block = block.reshape((2,) * len(bits) + (rows, groups, unit))
    for left in range(len(bits) - 1, -1, -1):
        mine = my_bit(bits[left])
        other = flip(pick(block, 1 - mine, left), bits[left])
        block = jnp.stack(settle([pick(block, mine, left), other], [bits[left]]), axis=left + 2)
    return block.reshape(rows, groups * size * unit)


def pack_rows(parts, width):
    lead = parts[0].shape[0]
    rows = []
    for part in parts:
        flat = part.reshape(lead, -1)
        short = -flat.shape[1] % width
        rows.append(jnp.pad(flat, ((0, 0), (0, short))).reshape(lead, -1, width))
    packed = jnp.concatenate(rows, axis=1)
    return jnp.pad(packed, ((0, 0), (0, -packed.shape[1] % 16), (0, 0)))


def unpack_rows(packed, shapes):
    lead, width = packed.shape[0], packed.shape[2]
    parts, at = [], 0
    for shape in shapes:
        size = 1
        for extent in shape:
            size *= extent
        count = -(-size // width)
        flat = packed[:, at : at + count].reshape(lead, -1)[:, :size]
        parts.append(flat.reshape((lead,) + tuple(shape)))
        at += count
    return parts


KEY_BLOCK = 256


def span(first, last, at):
    begin = first[at] // 16 * 16
    return begin, (last[at] - begin + KEY_BLOCK - 1) // KEY_BLOCK


def load_stream(piece_refs, slots, stream, sems):
    rows = piece_refs[0].shape[0]
    copies = []
    for number, piece in enumerate(piece_refs):
        to = pl.multiple_of(slots[number] * rows, 16)
        copies.append(
            pltpu.make_async_copy(piece, stream.at[pl.ds(to, rows), :], sems.at[number])
        )
    for copy in copies:
        copy.start()
    filled = rows * len(piece_refs)
    stream[pl.ds(filled, KEY_BLOCK), :] = jnp.zeros((KEY_BLOCK, stream.shape[1]), stream.dtype)
    for copy in copies:
        copy.wait()


def across(matrix_a, matrix_b):
    return lax.dot_general(
        matrix_a, matrix_b, (((1,), (1,)), ((), ())), preferred_element_type=jnp.float32
    )


def down_rows(matrix_a, matrix_b):
    return lax.dot_general(
        matrix_a, matrix_b, (((0,), (0,)), ((), ())), preferred_element_type=jnp.float32
    )


def attend_kernel(piece_count, step_count, first, last, slots, query_ref, own_ref, *refs):
    piece_refs = refs[:piece_count]
    out_ref, lse_ref, stream, sems = refs[piece_count:]
    head_size = query_ref.shape[2]
    scale = head_size ** (-0.5)
    load_stream(piece_refs, slots, stream, sems)

    def item(at, carry):
        query = query_ref[at]
        own = own_ref[at]
        scores = across(query, own[:, :head_size]) * scale
        column = lax.broadcasted_iota(jnp.int32, (1, own.shape[0]), 1)
        scores = jnp.where(column < step_count, scores, -1e30)
        top = jnp.max(scores, axis=1, keepdims=True)
        probs = jnp.exp(scores - top)
        mass = jnp.sum(probs, axis=1, keepdims=True)
        held = product(probs.astype(jnp.bfloat16), own[:, head_size:])
        begin, blocks = span(first, last, at)

        def block(number, state):
            top, mass, held = state
            row = pl.multiple_of(begin + number * KEY_BLOCK, 16)
            pairs = stream[pl.ds(row, KEY_BLOCK), :]
            scores = across(query, pairs[:, :head_size]) * scale
            place = row + lax.broadcasted_iota(jnp.int32, (1, KEY_BLOCK), 1)
            live = (place >= first[at]) & (place < last[at])
            scores = jnp.where(live, scores, -1e30)
            top_new = jnp.maximum(top, jnp.max(scores, axis=1, keepdims=True))
            shrink = jnp.exp(top - top_new)
            probs = jnp.exp(scores - top_new)
            mass = mass * shrink + jnp.sum(probs, axis=1, keepdims=True)
            held = held * shrink + product(probs.astype(jnp.bfloat16), pairs[:, head_size:])
            return top_new, mass, held

        top, mass, held = lax.fori_loop(0, blocks, block, (top, mass, held))
        out_ref[at] = (held / mass).astype(out_ref.dtype)
        lse_ref[at] = top + jnp.log(mass)
        return carry

    lax.fori_loop(0, query_ref.shape[0], item, 0)


def attend(pieces, slots, first, last, queries, own, step_count):
    items, rows, head_size = queries.shape
    stream_rows = len(pieces) * pieces[0].shape[0] + KEY_BLOCK
    scalars = pl.BlockSpec(memory_space=pltpu.SMEM)
    whole = pl.BlockSpec(memory_space=pltpu.VMEM)
    far = pl.BlockSpec(memory_space=pl.ANY)
    return pl.pallas_call(
        functools.partial(attend_kernel, len(pieces), step_count),
        out_shape=(
            jax.ShapeDtypeStruct(queries.shape, jnp.bfloat16),
            jax.ShapeDtypeStruct((items, rows, 1), jnp.float32),
        ),
        in_specs=[scalars] * 3 + [whole] * 2 + [far] * len(pieces),
        out_specs=(whole, whole),
        scratch_shapes=[
            pltpu.VMEM((stream_rows, 2 * head_size), jnp.bfloat16),
            pltpu.SemaphoreType.DMA((len(pieces),)),
        ],
        compiler_params=pltpu.CompilerParams(vmem_limit_bytes=KERNEL_BYTES),
        cost_estimate=pl.CostEstimate(
            flops=4 * items * rows * PMAX * head_size,
            bytes_accessed=stream_rows * 4 * head_size,
            transcendentals=items * rows * PMAX,
        ),
        name="attend",
    )(first, last, slots, queries, own, *pieces)


def attend_back_kernel(piece_count, step_count, first, last, slots, *refs):
    query_ref, own_ref, grad_ref, out_ref, lse_ref = refs[:5]
    piece_refs = refs[5 : 5 + piece_count]
    grad_query_ref, grad_own_ref = refs[5 + piece_count : 7 + piece_count]
    spread_refs = refs[7 + piece_count : 7 + 2 * piece_count]
    stream, spread, sems = refs[7 + 2 * piece_count :]
    head_size = query_ref.shape[2]
    scale = head_size ** (-0.5)
    chunk = piece_refs[0].shape[0]

    def clear(number, carry):
        row = pl.multiple_of(number * KEY_BLOCK, KEY_BLOCK)
        spread[pl.ds(row, KEY_BLOCK), :] = jnp.zeros((KEY_BLOCK, spread.shape[1]), spread.dtype)
        return carry

    lax.fori_loop(0, spread.shape[0] // KEY_BLOCK, clear, 0)
    load_stream(piece_refs, slots, stream, sems)

    def item(at, carry):
        query = query_ref[at]
        grad = grad_ref[at]
        lse = lse_ref[at]
        mean = jnp.sum(
            grad.astype(jnp.float32) * out_ref[at].astype(jnp.float32), axis=1, keepdims=True
        )

        def pull(pairs, live):
            keys = pairs[:, :head_size]
            scores = across(query, keys) * scale
            probs = jnp.where(live, jnp.exp(scores - lse), 0.0)
            grad_probs = across(grad, pairs[:, head_size:])
            grad_scores = (probs * (grad_probs - mean)).astype(jnp.bfloat16)
            grad_values = down_rows(probs.astype(jnp.bfloat16), grad)
            grad_keys = down_rows(grad_scores, query) * scale
            return (
                product(grad_scores, keys),
                grad_keys.astype(jnp.bfloat16),
                grad_values.astype(jnp.bfloat16),
            )

        own = own_ref[at]
        column = lax.broadcasted_iota(jnp.int32, (1, own.shape[0]), 1)
        grad_query, grad_keys, grad_values = pull(own, column < step_count)
        grad_own_ref[at, :, :head_size] = grad_keys
        grad_own_ref[at, :, head_size:] = grad_values
        begin, blocks = span(first, last, at)

        def block(number, grad_query):
            row = pl.multiple_of(begin + number * KEY_BLOCK, 16)
            place = row + lax.broadcasted_iota(jnp.int32, (1, KEY_BLOCK), 1)
            live = (place >= first[at]) & (place < last[at])
            more, grad_keys, grad_values = pull(stream[pl.ds(row, KEY_BLOCK), :], live)
            spread[pl.ds(row, KEY_BLOCK), :head_size] += grad_keys
            spread[pl.ds(row, KEY_BLOCK), head_size:] += grad_values
            return grad_query + more

        grad_query = lax.fori_loop(0, blocks, block, grad_query)
        grad_query_ref[at] = (grad_query * scale).astype(grad_query_ref.dtype)
        return carry

    lax.fori_loop(0, query_ref.shape[0], item, 0)
    copies = []
    for number, piece in enumerate(spread_refs):
        row = pl.multiple_of(slots[number] * chunk, 16)
        copies.append(
            pltpu.make_async_copy(spread.at[pl.ds(row, chunk), :], piece, sems.at[number])
        )
    for copy in copies:
        copy.start()
    for copy in copies:
        copy.wait()


def attend_back(pieces, slots, first, last, queries, own, grad, out, lse, step_count):
    items, rows, head_size = queries.shape
    chunk = pieces[0].shape[0]
    stream_rows = len(pieces) * chunk + KEY_BLOCK
    scalars = pl.BlockSpec(memory_space=pltpu.SMEM)
    whole = pl.BlockSpec(memory_space=pltpu.VMEM)
    far = pl.BlockSpec(memory_space=pl.ANY)
    return pl.pallas_call(
        functools.partial(attend_back_kernel, len(pieces), step_count),
        out_shape=(
            jax.ShapeDtypeStruct(queries.shape, jnp.bfloat16),
            jax.ShapeDtypeStruct(own.shape, jnp.bfloat16),
        )
        + (jax.ShapeDtypeStruct(pieces[0].shape, jnp.bfloat16),) * len(pieces),
        in_specs=[scalars] * 3 + [whole] * 5 + [far] * len(pieces),
        out_specs=(whole, whole) + (far,) * len(pieces),
        scratch_shapes=[
            pltpu.VMEM((stream_rows, 2 * head_size), jnp.bfloat16),
            pltpu.VMEM((stream_rows, 2 * head_size), jnp.bfloat16),
            pltpu.SemaphoreType.DMA((len(pieces),)),
        ],
        compiler_params=pltpu.CompilerParams(vmem_limit_bytes=KERNEL_BYTES),
        cost_estimate=pl.CostEstimate(
            flops=10 * items * rows * PMAX * head_size,
            bytes_accessed=stream_rows * 8 * head_size,
            transcendentals=items * rows * PMAX,
        ),
        name="attend_back",
    )(first, last, slots, queries, own, grad, out, lse, *pieces)


def on_device(
    prefix_rows,
    item_lengths,
    action_stretch,
    flow_noise,
    flow_times,
    action_dims,
    norm_gains,
    norm_gains_first,
    norm_gains_second,
    prefix_kv,
    prefix_kv_first,
    prefix_kv_second,
    action_in,
    action_in_first,
    action_in_second,
    action_qkv,
    action_qkv_first,
    action_qkv_second,
    attn_out,
    attn_out_first,
    attn_out_second,
    action_gate_up,
    action_gate_up_first,
    action_gate_up_second,
    action_down,
    action_down_first,
    action_down_second,
    action_head,
    action_head_first,
    action_head_second,
):
    masters = (
        norm_gains,
        prefix_kv,
        action_in,
        action_qkv,
        attn_out,
        action_gate_up,
        action_down,
        action_head,
    )
    moments_one = (
        norm_gains_first,
        prefix_kv_first,
        action_in_first,
        action_qkv_first,
        attn_out_first,
        action_gate_up_first,
        action_down_first,
        action_head_first,
    )
    moments_two = (
        norm_gains_second,
        prefix_kv_second,
        action_in_second,
        action_qkv_second,
        attn_out_second,
        action_gate_up_second,
        action_down_second,
        action_head_second,
    )
    inner_width = action_down.shape[1]
    devices = device_count()
    group = act_count()
    low_precision = jnp.bfloat16

    dims_sum = jnp.sum(action_dims).astype(jnp.float32).reshape(1, 1)
    small_shards = (prefix_kv, action_in, action_head, norm_gains)
    small_shapes = [part.shape for part in small_shards]
    pack_width = prefix_kv.shape[1]
    small = pack_rows(
        [part.astype(low_precision)[None] for part in small_shards + (dims_sum,)], pack_width
    )[0]
    small = fetch(small, far_bits())
    small = fetch(small, [near_bit()] + row_bits()).swapaxes(0, 1)
    small = double(small, CORE, 2)
    small_all = unpack_rows(
        small.reshape((devices,) + small.shape[-2:]), small_shapes + [(1, 1)]
    )
    kv_proj, in_proj, out_proj, gains_all = (
        part.reshape((-1,) + part.shape[2:]) for part in small_all[:4]
    )
    counted = jnp.float32(action_stretch.shape[1]) * jnp.sum(small_all[4].astype(jnp.float32))

    hidden_width = action_gate_up.shape[1] // 2
    unit_block = action_down.shape[0]
    unit_groups = 2 * hidden_width // (group * unit_block)
    side_width = unit_groups * unit_block
    sides = swap_in(
        action_gate_up.astype(low_precision).reshape(-1, unit_groups, group, unit_block)
    )
    side_rows = sides.shape[0]
    layer = jnp.concatenate([sides, action_down.astype(low_precision).reshape(-1, side_width)])
    layer = lax.all_gather(layer, "wide", axis=0)
    gate_up_proj = layer[:, :side_rows].reshape(inner_width, side_width)
    down_proj = layer[:, side_rows:].reshape(side_width // 2, inner_width)

    attn_weights = []
    for part in (action_qkv, attn_out):
        block = collect_plane(fetch(part.astype(low_precision), far_bits()))
        block = double(block, CORE, -3)
        attn_weights.append(block.reshape(-1, part.shape[1]))
    qkv_proj, out_att = attn_weights

    model_width = prefix_rows.shape[1]
    query_width = out_att.shape[0]
    head_size = (qkv_proj.shape[1] - query_width) // 2
    head_count = query_width // head_size
    item_count, step_count, action_width = action_stretch.shape
    row_count = item_count * step_count
    gain_pre, gain_one, gain_two, gain_three = split_gains(gains_all, model_width, inner_width)
    pre_normed, pre_unit, pre_inverse = norm_forward(prefix_rows.astype(jnp.float32), gain_pre)
    pre_in = pre_normed.astype(low_precision)
    pre_keys = product(pre_in, kv_proj).astype(low_precision)
    act_rank = lax.axis_index(("row", "core"))
    pieces = [pre_keys]
    piece_ranks = [0]
    for bit in row_bits() + [CORE]:
        pieces += [flip(piece, bit) for piece in pieces]
        piece_ranks += [rank + bit for rank in piece_ranks]
    slots = jnp.stack([act_rank ^ rank for rank in piece_ranks])
    ends_at = jnp.cumsum(item_lengths[0])
    mine_end = lax.dynamic_slice_in_dim(ends_at, act_rank * item_count, item_count)
    mine_start = lax.dynamic_slice_in_dim(
        ends_at - item_lengths[0], act_rank * item_count, item_count
    )
    blend_t = flow_times[:, None, None]
    noisy_acts = blend_t * flow_noise + (1.0 - blend_t) * action_stretch
    stamp_feats = jnp.broadcast_to(
        time_features(flow_times, TFEAT)[:, None, :], (item_count, step_count, TFEAT)
    )
    features = (
        jnp.concatenate([noisy_acts, stamp_feats], axis=2)
        .reshape(row_count, -1)
        .astype(low_precision)
    )
    base_res = product(features, in_proj)
    attn_normed, unit_one, inverse_one = norm_forward(base_res, gain_one)
    attn_in = attn_normed.astype(low_precision)
    projected = product(attn_in, qkv_proj)
    item_rows = (item_count, step_count * head_count, head_size)
    queries = projected[:, :query_width].astype(low_precision).reshape(item_rows)
    own_kv = (
        projected[:, query_width:]
        .astype(low_precision)
        .reshape(item_count, step_count, 2 * head_size)
    )
    own_kv = jnp.pad(own_kv, ((0, 0), (0, -step_count % 64), (0, 0)))
    attended_rows, lse = attend(
        pieces, slots, mine_start, mine_end, queries, own_kv, step_count
    )
    attended = attended_rows.reshape(row_count, query_width)
    mid_res = base_res + product(attended, out_att)
    mlp_normed, unit_two, inverse_two = norm_forward(mid_res, gain_two)
    mlp_in = mlp_normed.astype(low_precision)
    mlp_all = share_rows(mlp_in)
    gate_vals = product(mlp_all, gate_up_proj)
    half_side = side_width // 2
    gate_part, up_part = gate_vals[:, :half_side], gate_vals[:, half_side:]
    hidden = glu_unit(gate_part, up_part).astype(low_precision)
    top_res = mid_res + return_rows(product(hidden, down_proj))
    head_normed, unit_three, inverse_three = norm_forward(top_res, gain_three)
    head_in = head_normed.astype(low_precision)
    predicted = product(head_in, out_proj).reshape(item_count, step_count, action_width)
    keep_dims = (jnp.arange(action_width)[None, :] < action_dims[:, None]).astype(jnp.float32)
    mismatch = (predicted - (flow_noise - action_stretch)) * keep_dims[:, None, :]
    loss_local = jnp.sum(mismatch * mismatch)

    grad_pred = (2.0 * mismatch / counted).reshape(row_count, -1).astype(low_precision)
    grad_head = product(head_in.T, grad_pred)
    grad_top, gain_grad_three = norm_backward(
        product(grad_pred, out_proj.T), unit_three, inverse_three, gain_three
    )
    grad_mlp = grad_top.astype(low_precision)
    grad_mlp_all = share_rows(grad_mlp)
    grad_down = product(hidden.T, grad_mlp_all).astype(low_precision)
    grad_down = lax.psum_scatter(grad_down, "wide", scatter_dimension=0, tiled=True)
    grad_hidden = product(grad_mlp_all, down_proj.T)
    glu_value, glu_pull = jax.vjp(glu_unit, gate_part, up_part)
    grad_gate_up = jnp.concatenate(glu_pull(grad_hidden), axis=1).astype(low_precision)
    grad_sides = product(mlp_all.T, grad_gate_up).astype(low_precision)
    grad_sides = lax.psum_scatter(grad_sides, "wide", scatter_dimension=0, tiled=True)
    grad_mlp_in = return_rows(product(grad_gate_up, gate_up_proj.T))
    grad_gate_up = swap_out(grad_sides, unit_groups)
    grad_mlp_in, gain_grad_two = norm_backward(grad_mlp_in, unit_two, inverse_two, gain_two)
    grad_mid = grad_top + grad_mlp_in
    grad_branch = grad_mid.astype(low_precision)
    grad_out_att = product(attended.T, grad_branch).astype(low_precision)
    grad_out_att = disperse(grad_out_att.reshape((devices,) + attn_out.shape))
    grad_attended = product(grad_branch, out_att.T).astype(low_precision).reshape(item_rows)
    grad_queries, grad_own, *spread = attend_back(
        pieces,
        slots,
        mine_start,
        mine_end,
        queries,
        own_kv,
        grad_attended,
        attended_rows,
        lse,
        step_count,
    )
    grad_projected = jnp.concatenate(
        [
            grad_queries.reshape(row_count, query_width),
            grad_own[:, :step_count].reshape(row_count, 2 * head_size),
        ],
        axis=1,
    )
    grad_qkv = product(attn_in.T, grad_projected).astype(low_precision)
    grad_qkv = disperse(grad_qkv.reshape((devices,) + action_qkv.shape))
    grad_attn_in, gain_grad_one = norm_backward(
        product(grad_projected, qkv_proj.T), unit_one, inverse_one, gain_one
    )
    grad_base = (grad_mid + grad_attn_in).astype(low_precision)
    grad_in = product(features.T, grad_base)
    for bit in [CORE] + row_bits()[::-1]:
        half = len(spread) // 2
        spread = [
            piece + flip(other, bit) for piece, other in zip(spread[:half], spread[half:])
        ]
    grad_prefix = spread[0]
    grad_kv = product(pre_in.T, grad_prefix)
    gain_grad_pre = jnp.sum(grad_kv * kv_proj.astype(jnp.float32), axis=1) / gain_pre
    grad_gains = jnp.concatenate([gain_grad_pre, gain_grad_one, gain_grad_two, gain_grad_three])
    small_grads = [
        part.astype(low_precision).reshape((devices,) + shard.shape)
        for part, shard in zip((grad_kv, grad_in, grad_head, grad_gains), small_shards)
    ]
    small_grads = pack_rows(small_grads, pack_width)
    small_grads = disperse_small(small_grads)
    small_grads = unpack_rows(small_grads[None], small_shapes)
    grad_kv, grad_in, grad_head, grad_gains = (part[0] for part in small_grads)
    gradients = (
        grad_gains,
        grad_kv,
        grad_in,
        grad_qkv,
        grad_out_att,
        grad_gate_up.astype(jnp.float32),
        grad_down.astype(jnp.float32),
        grad_head,
    )
    local_squares = sum((jnp.sum(grad_one * grad_one) for grad_one in gradients))
    sums = total(jnp.stack([loss_local, local_squares]))
    loss_sum = sums[0]
    grad_norm = jnp.sqrt(sums[1])
    clip_factor = jnp.minimum(1.0, CLIP_AT / (grad_norm + 1e-06))
    step_rates = (GAIN_RATE,) + (MATRIX_RATE,) * 7
    decay_rates = (0.0,) + (WEIGHT_DECAY,) * 7
    updated = []
    for master_w, moment_one, moment_two, gradient, step_rate, decay_rate in zip(
        masters, moments_one, moments_two, gradients, step_rates, decay_rates
    ):
        updated.extend(
            adamw(master_w, moment_one, moment_two, gradient * clip_factor, step_rate, decay_rate)
        )
    return (
        updated[0],
        updated[1],
        updated[2],
        updated[3],
        updated[4],
        updated[5],
        updated[6],
        updated[7],
        updated[8],
        updated[9],
        updated[10],
        updated[11],
        updated[12],
        updated[13],
        updated[14],
        updated[15],
        updated[16],
        updated[17],
        updated[18],
        updated[19],
        updated[20],
        updated[21],
        updated[22],
        updated[23],
        loss_sum,
        counted,
        grad_norm,
    )


def solution(mesh):
    wide, act = mesh.devices.shape
    lanes_mesh = Mesh(mesh.devices.reshape(wide, act // 2, 2), AXES)
    placed = (
        P(AXES, None),
        P("wide", None),
        P(AXES, None, None),
        P(AXES, None, None),
        P(AXES),
        P(AXES),
        P(AXES),
        P(AXES),
        P(AXES),
        P(AXES, None),
        P(AXES, None),
        P(AXES, None),
        P(AXES, None),
        P(AXES, None),
        P(AXES, None),
        P(AXES, None),
        P(AXES, None),
        P(AXES, None),
        P(AXES, None),
        P(AXES, None),
        P(AXES, None),
        P(AXES, None),
        P(AXES, None),
        P(AXES, None),
        P(AXES, None),
        P(AXES, None),
        P(AXES, None),
        P(AXES, None),
        P(AXES, None),
        P(AXES, None),
    )
    return jax.shard_map(
        on_device,
        mesh=lanes_mesh,
        in_specs=placed,
        out_specs=(
            P(AXES),
            P(AXES),
            P(AXES),
            P(AXES, None),
            P(AXES, None),
            P(AXES, None),
            P(AXES, None),
            P(AXES, None),
            P(AXES, None),
            P(AXES, None),
            P(AXES, None),
            P(AXES, None),
            P(AXES, None),
            P(AXES, None),
            P(AXES, None),
            P(AXES, None),
            P(AXES, None),
            P(AXES, None),
            P(AXES, None),
            P(AXES, None),
            P(AXES, None),
            P(AXES, None),
            P(AXES, None),
            P(AXES, None),
            P(),
            P(),
            P(),
        ),
        check_vma=False,
    )
```

```python
import functools

import jax
import jax.numpy as jnp
from jax import lax
from jax.experimental import pallas as pl
from jax.experimental.pallas import tpu as pltpu
from jax.sharding import Mesh
from jax.sharding import PartitionSpec as P

TFEAT = 96
PMAX = 1024
STEP = 10
KERNEL_BYTES = 48 * 1024 * 1024


NORM_EPS = 1e-06
CLIP_AT = 0.005
BETA_ONE = 0.9
BETA_TWO = 0.95
ADAM_EPS = 1e-08
MATRIX_RATE = 0.02
GAIN_RATE = 0.7
WEIGHT_DECAY = 0.01


def product(matrix_a, matrix_b):
    return jnp.dot(matrix_a, matrix_b, preferred_element_type=jnp.float32)


def norm_forward(values, scaling):
    inverse = lax.rsqrt(jnp.mean(values * values, axis=-1, keepdims=True) + NORM_EPS)
    unit_vals = values * inverse
    return (unit_vals * scaling, unit_vals, inverse)


def norm_backward(grad_out, unit_vals, inverse, scaling):
    grad_unit = grad_out * scaling
    grad_in = inverse * (
        grad_unit - unit_vals * jnp.mean(grad_unit * unit_vals, axis=-1, keepdims=True)
    )
    return (grad_in, jnp.sum(grad_out * unit_vals, axis=0))


def time_features(stamps, feat_width):
    half_width = feat_width // 2
    ladder = jnp.arange(half_width, dtype=jnp.float32) / (half_width - 1)
    frequency = 6.283185307179586 / (0.004 * 1000.0**ladder)
    angles = stamps[:, None] * frequency[None, :]
    return jnp.concatenate([jnp.sin(angles), jnp.cos(angles)], axis=1)


def glu_unit(gate_in, up_in):
    return jax.nn.gelu(gate_in, approximate=True) * up_in


def adamw(master_w, moment_one, moment_two, gradient, step_rate, decay_rate):
    first_new = BETA_ONE * moment_one + (1.0 - BETA_ONE) * gradient
    second_new = BETA_TWO * moment_two + (1.0 - BETA_TWO) * gradient * gradient
    first_hat = first_new / (1.0 - BETA_ONE**STEP)
    second_hat = second_new / (1.0 - BETA_TWO**STEP)
    master_new = master_w - step_rate * (
        first_hat / (jnp.sqrt(second_hat) + ADAM_EPS) + decay_rate * master_w
    )
    return (master_new, first_new, second_new)


def split_gains(gains_all, model_width, inner_width):
    gains_f = gains_all.astype(jnp.float32)
    return (
        gains_f[:model_width],
        gains_f[model_width : model_width + inner_width],
        gains_f[model_width + inner_width : model_width + 2 * inner_width],
        gains_f[model_width + 2 * inner_width :],
    )


AXES = ("wide", "row", "core")
CORE = 1


def device_count():
    return lax.axis_size(AXES)


def act_count():
    return lax.axis_size(("row", "core"))


def flip(block, mask):
    return lax.ppermute(block, AXES, [(place, place ^ mask) for place in range(device_count())])


def my_bit(mask):
    return (lax.axis_index(AXES) // mask) % 2


def bits_between(low, high):
    bits = []
    while low < high:
        bits.append(low)
        low *= 2
    return bits[::-1]


def row_bits():
    return bits_between(2, act_count())


def near_bit():
    return act_count()


def far_bits():
    return bits_between(2 * act_count(), device_count())


def combos(bits):
    masks = [0]
    for bit in bits:
        masks = [mask + more for mask in masks for more in (0, bit)]
    return masks


def settle(blocks, bits):
    for number, bit in enumerate(bits):
        step = len(blocks) >> (number + 1)
        swap = my_bit(bit) == 1
        blocks = [jnp.where(swap, blocks[at ^ step], blocks[at]) for at in range(len(blocks))]
    return blocks


def after(block, *others):
    return lax.optimization_barrier((block,) + others)[0]


def fetch(block, bits, *others):
    blocks = [block if mask == 0 else flip(block, mask) for mask in combos(bits)]
    if others:
        blocks = lax.optimization_barrier((blocks,) + others)[0]
    return jnp.stack(settle(blocks, bits))


def double(block, bit, at, *others):
    other = flip(block, bit)
    if others:
        other = after(other, *others)
    return jnp.stack(settle([block, other], [bit]), axis=at)


def place_index(bits):
    index = 0
    for bit in bits:
        index = 2 * index + my_bit(bit)
    return index


def pick(block, index, at):
    return lax.dynamic_index_in_dim(block, index, at, keepdims=False)


def wide_sum(blocks):
    return sum(block.astype(jnp.float32) for block in blocks)


def part_ways(block, bit, at):
    mine = my_bit(bit)
    return pick(block, 1 - mine, at), pick(block, mine, at)


def meet(send, keep, bit, *others):
    other = flip(send, bit)
    if others:
        other = after(other, *others)
    return wide_sum([keep, other]).astype(jnp.bfloat16)


def halve(block, bit, at, *others):
    return meet(*part_ways(block, bit, at), bit, *others)


def hand_out(block, bits, *others):
    mine = place_index(bits)
    blocks = [pick(block, mine, 0)]
    for number, mask in enumerate(combos(bits)):
        if mask:
            blocks.append(flip(pick(block, mine ^ number, 0), mask))
    if others:
        blocks = lax.optimization_barrier((blocks,) + others)[0]
    return wide_sum(blocks)


def core_sum(block):
    rows, columns = block.shape[1:]
    far = 2 ** len(far_bits())
    block = halve(block.reshape(-1, 2, rows, columns), CORE, 1)
    return block.reshape((far, 2) + (2,) * len(row_bits()) + (rows, columns))


def row_sum(block):
    for bit in row_bits():
        block = halve(block, bit, 2)
    return block


def total(value):
    for bit in bits_between(1, device_count())[::-1]:
        value = value + flip(value, bit)
    return value


def trade_list(block, pairs):
    group = act_count()
    return lax.ppermute(
        block,
        AXES,
        [
            (start + sender, start + receiver)
            for start in range(0, device_count(), group)
            for sender, receiver in pairs
        ],
    )


def share_rows(block):
    for bit in row_bits() + [CORE]:
        block = jnp.concatenate([block, flip(block, bit)])
    return block


def return_rows(block):
    for bit in [CORE] + row_bits()[::-1]:
        half = block.shape[0] // 2
        other = flip(block[half:].astype(jnp.bfloat16), bit)
        block = block[:half] + other.astype(jnp.float32)
    return block


def swap_in(block):
    rows, groups, size, unit = block.shape
    bits = row_bits() + [CORE]
    block = block.reshape((rows, groups) + (2,) * len(bits) + (unit,))
    for done, bit in enumerate(bits):
        mine = my_bit(bit)
        other = flip(pick(block, 1 - mine, done + 2), bit)
        block = jnp.stack(settle([pick(block, mine, done + 2), other], [bit]), axis=done)
    return block.reshape(size * rows, groups * unit)


def swap_out(block, groups):
    bits = row_bits() + [CORE]
    size = act_count()
    rows, unit = block.shape[0] // size, block.shape[1] // groups
    block = block.reshape((2,) * len(bits) + (rows, groups, unit))
    for left in range(len(bits) - 1, -1, -1):
        mine = my_bit(bits[left])
        other = flip(pick(block, 1 - mine, left), bits[left])
        block = jnp.stack(settle([pick(block, mine, left), other], [bits[left]]), axis=left + 2)
    return block.reshape(rows, groups * size * unit)


def pack_rows(parts, width):
    lead = parts[0].shape[0]
    rows = []
    for part in parts:
        flat = part.reshape(lead, -1)
        short = -flat.shape[1] % width
        rows.append(jnp.pad(flat, ((0, 0), (0, short))).reshape(lead, -1, width))
    packed = jnp.concatenate(rows, axis=1)
    return jnp.pad(packed, ((0, 0), (0, -packed.shape[1] % 16), (0, 0)))


def unpack_rows(packed, shapes):
    lead, width = packed.shape[0], packed.shape[2]
    parts, at = [], 0
    for shape in shapes:
        size = 1
        for extent in shape:
            size *= extent
        count = -(-size // width)
        flat = packed[:, at : at + count].reshape(lead, -1)[:, :size]
        parts.append(flat.reshape((lead,) + tuple(shape)))
        at += count
    return parts


KEY_BLOCK = 256


def span(first, last, at):
    begin = first[at] // 16 * 16
    return begin, (last[at] - begin + KEY_BLOCK - 1) // KEY_BLOCK


def load_stream(piece_refs, offsets, stream, sems):
    count = len(piece_refs)
    for number in range(count, offsets.shape[0]):
        row = pl.multiple_of(offsets[number], 16)
        stream[pl.ds(row, KEY_BLOCK), :] = jnp.zeros((KEY_BLOCK, stream.shape[1]), stream.dtype)
    copies = []
    for number, piece in enumerate(piece_refs):
        row = pl.multiple_of(offsets[number], 16)
        copies.append(
            pltpu.make_async_copy(
                piece, stream.at[pl.ds(row, piece.shape[0]), :], sems.at[number]
            )
        )
    for copy in copies:
        copy.start()
    for copy in copies:
        copy.wait()


def across(matrix_a, matrix_b):
    return lax.dot_general(
        matrix_a, matrix_b, (((1,), (1,)), ((), ())), preferred_element_type=jnp.float32
    )


def down_rows(matrix_a, matrix_b):
    return lax.dot_general(
        matrix_a, matrix_b, (((0,), (0,)), ((), ())), preferred_element_type=jnp.float32
    )


def attend_kernel(piece_count, step_count, first, last, offsets, query_ref, own_ref, *refs):
    piece_refs = refs[:piece_count]
    out_ref, lse_ref, stream, sems = refs[piece_count:]
    head_size = query_ref.shape[2]
    scale = head_size ** (-0.5)
    load_stream(piece_refs, offsets, stream, sems)

    def item(at, carry):
        query = query_ref[at]
        own = own_ref[at]
        scores = across(query, own[:, :head_size]) * scale
        column = lax.broadcasted_iota(jnp.int32, (1, own.shape[0]), 1)
        scores = jnp.where(column < step_count, scores, -1e30)
        top = jnp.max(scores, axis=1, keepdims=True)
        probs = jnp.exp(scores - top)
        mass = jnp.sum(probs, axis=1, keepdims=True)
        held = product(probs.astype(jnp.bfloat16), own[:, head_size:])
        begin, blocks = span(first, last, at)

        def block(number, state):
            top, mass, held = state
            row = pl.multiple_of(begin + number * KEY_BLOCK, 16)
            pairs = stream[pl.ds(row, KEY_BLOCK), :]
            scores = across(query, pairs[:, :head_size]) * scale
            place = row + lax.broadcasted_iota(jnp.int32, (1, KEY_BLOCK), 1)
            live = (place >= first[at]) & (place < last[at])
            scores = jnp.where(live, scores, -1e30)
            top_new = jnp.maximum(top, jnp.max(scores, axis=1, keepdims=True))
            shrink = jnp.exp(top - top_new)
            probs = jnp.exp(scores - top_new)
            mass = mass * shrink + jnp.sum(probs, axis=1, keepdims=True)
            held = held * shrink + product(probs.astype(jnp.bfloat16), pairs[:, head_size:])
            return top_new, mass, held

        top, mass, held = lax.fori_loop(0, blocks, block, (top, mass, held))
        out_ref[at] = (held / mass).astype(out_ref.dtype)
        lse_ref[at] = top + jnp.log(mass)
        return carry

    lax.fori_loop(0, query_ref.shape[0], item, 0)


def attend(pieces, offsets, first, last, queries, own, step_count, stream_len):
    items, rows, head_size = queries.shape
    stream_rows = stream_len + KEY_BLOCK
    scalars = pl.BlockSpec(memory_space=pltpu.SMEM)
    whole = pl.BlockSpec(memory_space=pltpu.VMEM)
    far = pl.BlockSpec(memory_space=pl.ANY)
    return pl.pallas_call(
        functools.partial(attend_kernel, len(pieces), step_count),
        out_shape=(
            jax.ShapeDtypeStruct(queries.shape, jnp.bfloat16),
            jax.ShapeDtypeStruct((items, rows, 1), jnp.float32),
        ),
        in_specs=[scalars] * 3 + [whole] * 2 + [far] * len(pieces),
        out_specs=(whole, whole),
        scratch_shapes=[
            pltpu.VMEM((stream_rows, 2 * head_size), jnp.bfloat16),
            pltpu.SemaphoreType.DMA((len(pieces),)),
        ],
        compiler_params=pltpu.CompilerParams(vmem_limit_bytes=KERNEL_BYTES),
        cost_estimate=pl.CostEstimate(flops=1, bytes_accessed=1, transcendentals=0),
        name="attend",
    )(first, last, offsets, queries, own, *pieces)


def attend_back_kernel(piece_count, step_count, first, last, offsets, *refs):
    query_ref, own_ref, grad_ref, out_ref, lse_ref = refs[:5]
    piece_refs = refs[5 : 5 + piece_count]
    grad_query_ref, grad_own_ref = refs[5 + piece_count : 7 + piece_count]
    spread_refs = refs[7 + piece_count : 7 + 2 * piece_count]
    stream, spread, sems = refs[7 + 2 * piece_count :]
    head_size = query_ref.shape[2]
    scale = head_size ** (-0.5)

    def clear(number, carry):
        row = pl.multiple_of(number * KEY_BLOCK, KEY_BLOCK)
        spread[pl.ds(row, KEY_BLOCK), :] = jnp.zeros((KEY_BLOCK, spread.shape[1]), spread.dtype)
        return carry

    lax.fori_loop(0, spread.shape[0] // KEY_BLOCK, clear, 0)
    load_stream(piece_refs, offsets, stream, sems)

    def item(at, carry):
        query = query_ref[at]
        grad = grad_ref[at]
        lse = lse_ref[at]
        mean = jnp.sum(
            grad.astype(jnp.float32) * out_ref[at].astype(jnp.float32), axis=1, keepdims=True
        )

        def pull(pairs, live):
            keys = pairs[:, :head_size]
            scores = across(query, keys) * scale
            probs = jnp.where(live, jnp.exp(scores - lse), 0.0)
            grad_probs = across(grad, pairs[:, head_size:])
            grad_scores = (probs * (grad_probs - mean)).astype(jnp.bfloat16)
            grad_values = down_rows(probs.astype(jnp.bfloat16), grad)
            grad_keys = down_rows(grad_scores, query) * scale
            return (
                product(grad_scores, keys),
                grad_keys.astype(jnp.bfloat16),
                grad_values.astype(jnp.bfloat16),
            )

        own = own_ref[at]
        column = lax.broadcasted_iota(jnp.int32, (1, own.shape[0]), 1)
        grad_query, grad_keys, grad_values = pull(own, column < step_count)
        grad_own_ref[at, :, :head_size] = grad_keys
        grad_own_ref[at, :, head_size:] = grad_values
        begin, blocks = span(first, last, at)

        def block(number, grad_query):
            row = pl.multiple_of(begin + number * KEY_BLOCK, 16)
            place = row + lax.broadcasted_iota(jnp.int32, (1, KEY_BLOCK), 1)
            live = (place >= first[at]) & (place < last[at])
            more, grad_keys, grad_values = pull(stream[pl.ds(row, KEY_BLOCK), :], live)
            spread[pl.ds(row, KEY_BLOCK), :head_size] += grad_keys
            spread[pl.ds(row, KEY_BLOCK), head_size:] += grad_values
            return grad_query + more

        grad_query = lax.fori_loop(0, blocks, block, grad_query)
        grad_query_ref[at] = (grad_query * scale).astype(grad_query_ref.dtype)
        return carry

    lax.fori_loop(0, query_ref.shape[0], item, 0)
    copies = []
    for number, piece in enumerate(spread_refs):
        row = pl.multiple_of(offsets[number], 16)
        copies.append(
            pltpu.make_async_copy(
                spread.at[pl.ds(row, piece.shape[0]), :], piece, sems.at[number]
            )
        )
    for copy in copies:
        copy.start()
    for copy in copies:
        copy.wait()


def attend_back(pieces, offsets, first, last, queries, own, grad, out, lse, step_count, stream_len):
    items, rows, head_size = queries.shape
    stream_rows = stream_len + KEY_BLOCK
    scalars = pl.BlockSpec(memory_space=pltpu.SMEM)
    whole = pl.BlockSpec(memory_space=pltpu.VMEM)
    far = pl.BlockSpec(memory_space=pl.ANY)
    return pl.pallas_call(
        functools.partial(attend_back_kernel, len(pieces), step_count),
        out_shape=(
            jax.ShapeDtypeStruct(queries.shape, jnp.bfloat16),
            jax.ShapeDtypeStruct(own.shape, jnp.bfloat16),
        )
        + tuple(jax.ShapeDtypeStruct(piece.shape, jnp.bfloat16) for piece in pieces),
        in_specs=[scalars] * 3 + [whole] * 5 + [far] * len(pieces),
        out_specs=(whole, whole) + (far,) * len(pieces),
        scratch_shapes=[
            pltpu.VMEM((stream_rows, 2 * head_size), jnp.bfloat16),
            pltpu.VMEM((stream_rows, 2 * head_size), jnp.bfloat16),
            pltpu.SemaphoreType.DMA((len(pieces),)),
        ],
        compiler_params=pltpu.CompilerParams(vmem_limit_bytes=KERNEL_BYTES),
        cost_estimate=pl.CostEstimate(flops=1, bytes_accessed=1, transcendentals=0),
        name="attend_back",
    )(first, last, offsets, queries, own, grad, out, lse, *pieces)


def on_device(
    prefix_rows,
    item_lengths,
    action_stretch,
    flow_noise,
    flow_times,
    action_dims,
    norm_gains,
    norm_gains_first,
    norm_gains_second,
    prefix_kv,
    prefix_kv_first,
    prefix_kv_second,
    action_in,
    action_in_first,
    action_in_second,
    action_qkv,
    action_qkv_first,
    action_qkv_second,
    attn_out,
    attn_out_first,
    attn_out_second,
    action_gate_up,
    action_gate_up_first,
    action_gate_up_second,
    action_down,
    action_down_first,
    action_down_second,
    action_head,
    action_head_first,
    action_head_second,
):
    masters = (
        norm_gains,
        prefix_kv,
        action_in,
        action_qkv,
        attn_out,
        action_gate_up,
        action_down,
        action_head,
    )
    moments_one = (
        norm_gains_first,
        prefix_kv_first,
        action_in_first,
        action_qkv_first,
        attn_out_first,
        action_gate_up_first,
        action_down_first,
        action_head_first,
    )
    moments_two = (
        norm_gains_second,
        prefix_kv_second,
        action_in_second,
        action_qkv_second,
        attn_out_second,
        action_gate_up_second,
        action_down_second,
        action_head_second,
    )
    inner_width = action_down.shape[1]
    devices = device_count()
    group = act_count()
    low_precision = jnp.bfloat16

    dims_sum = jnp.sum(action_dims).astype(jnp.float32).reshape(1, 1)
    small_shards = (prefix_kv, action_in, action_head, norm_gains)
    small_shapes = [part.shape for part in small_shards]
    pack_width = prefix_kv.shape[1]
    small = pack_rows(
        [part.astype(low_precision)[None] for part in small_shards + (dims_sum,)], pack_width
    )[0]
    small_far = fetch(small, far_bits())
    small = fetch(small_far, [near_bit()] + row_bits()).swapaxes(0, 1)
    small = double(small, CORE, 2)
    small_all = unpack_rows(
        small.reshape((devices,) + small.shape[-2:]), small_shapes + [(1, 1)]
    )
    kv_proj, in_proj, out_proj, gains_all = (
        part.reshape((-1,) + part.shape[2:]) for part in small_all[:4]
    )
    counted = jnp.float32(action_stretch.shape[1]) * jnp.sum(small_all[4].astype(jnp.float32))

    hidden_width = action_gate_up.shape[1] // 2
    unit_block = action_down.shape[0]
    unit_groups = 2 * hidden_width // (group * unit_block)
    side_width = unit_groups * unit_block
    sides = swap_in(
        action_gate_up.astype(low_precision).reshape(-1, unit_groups, group, unit_block)
    )
    side_rows = sides.shape[0]
    qkv_proj = lax.all_gather(action_qkv.astype(low_precision), AXES, axis=0, tiled=True)
    layer = jnp.concatenate(
        [sides, action_down.astype(low_precision).reshape(side_rows, -1)], axis=1
    )
    layer = lax.all_gather(layer, "wide", axis=0, tiled=True)
    gate_up_proj = layer[:, :side_width]
    down_proj = layer[:, side_width:].reshape(side_width // 2, inner_width)

    model_width = prefix_rows.shape[1]
    query_width = devices * attn_out.shape[0]
    head_size = (action_qkv.shape[1] - query_width) // 2
    head_count = query_width // head_size
    item_count, step_count, action_width = action_stretch.shape
    row_count = item_count * step_count
    gain_pre, gain_one, gain_two, gain_three = split_gains(gains_all, model_width, inner_width)
    pre_normed, pre_unit, pre_inverse = norm_forward(prefix_rows.astype(jnp.float32), gain_pre)
    pre_in = pre_normed.astype(low_precision)
    pre_keys = product(pre_in, kv_proj).astype(low_precision)
    act_rank = lax.axis_index(("row", "core"))
    chunk = pre_keys.shape[0]
    stream_len = group * chunk
    reach = action_stretch.shape[0] * PMAX
    tail = 2 * reach - 3 * chunk
    narrow = group == 4 and reach <= 2 * chunk and 0 < tail <= chunk and tail % 16 == 0
    if narrow:
        outer_end = jnp.where(act_rank == 0, pre_keys[chunk - tail :], pre_keys[:tail])
        pieces = [
            pre_keys,
            flip(pre_keys, CORE),
            trade_list(pre_keys, [(1, 2), (2, 1)]),
            trade_list(outer_end, [(3, 1), (0, 2)]),
        ]
        tail_at = pick(jnp.array([2 * chunk, 3 * chunk, chunk - tail, chunk]), act_rank, 0)
        offsets = jnp.stack(
            [
                act_rank * chunk,
                (act_rank ^ 1) * chunk,
                (3 - act_rank) * chunk,
                tail_at,
                jnp.full_like(tail_at, stream_len),
                jnp.full_like(tail_at, 3 * chunk + tail),
            ]
        )
    else:
        pieces = [pre_keys]
        ranks = [0]
        for bit in row_bits() + [CORE]:
            pieces += [flip(piece, bit) for piece in pieces]
            ranks += [rank + bit for rank in ranks]
        offsets = jnp.stack(
            [(act_rank ^ rank) * chunk for rank in ranks]
            + [jnp.full_like(act_rank, stream_len)]
        )

    ends_at = jnp.cumsum(item_lengths[0])
    mine_end = lax.dynamic_slice_in_dim(ends_at, act_rank * item_count, item_count)
    mine_start = lax.dynamic_slice_in_dim(
        ends_at - item_lengths[0], act_rank * item_count, item_count
    )
    blend_t = flow_times[:, None, None]
    noisy_acts = blend_t * flow_noise + (1.0 - blend_t) * action_stretch
    stamp_feats = jnp.broadcast_to(
        time_features(flow_times, TFEAT)[:, None, :], (item_count, step_count, TFEAT)
    )
    features = (
        jnp.concatenate([noisy_acts, stamp_feats], axis=2)
        .reshape(row_count, -1)
        .astype(low_precision)
    )
    base_res = product(features, in_proj)
    attn_normed, unit_one, inverse_one = norm_forward(base_res, gain_one)
    attn_in = attn_normed.astype(low_precision)
    projected = product(attn_in, qkv_proj)
    item_rows = (item_count, step_count * head_count, head_size)
    queries = projected[:, :query_width].astype(low_precision).reshape(item_rows)
    own_kv = (
        projected[:, query_width:]
        .astype(low_precision)
        .reshape(item_count, step_count, 2 * head_size)
    )
    own_kv = jnp.pad(own_kv, ((0, 0), (0, -step_count % 64), (0, 0)))
    out_att = fetch(after(attn_out.astype(low_precision), small), far_bits(), queries)
    out_att = after(double(out_att, near_bit(), 1), *pieces)
    attended_rows, lse = attend(
        pieces, offsets, mine_start, mine_end, after(queries, out_att), own_kv, step_count, stream_len
    )
    for bit in row_bits() + [CORE]:
        out_att = double(out_att, bit, -3, attended_rows)
    out_att = out_att.reshape(query_width, inner_width)
    attended = attended_rows.reshape(row_count, query_width)
    mid_res = base_res + product(attended, out_att)
    mlp_normed, unit_two, inverse_two = norm_forward(mid_res, gain_two)
    mlp_in = mlp_normed.astype(low_precision)
    mlp_all = share_rows(mlp_in)
    gate_vals = product(mlp_all, gate_up_proj)
    half_side = side_width // 2
    gate_part, up_part = gate_vals[:, :half_side], gate_vals[:, half_side:]
    hidden = glu_unit(gate_part, up_part).astype(low_precision)
    top_res = mid_res + return_rows(product(hidden, down_proj))
    head_normed, unit_three, inverse_three = norm_forward(top_res, gain_three)
    head_in = head_normed.astype(low_precision)
    predicted = product(head_in, out_proj).reshape(item_count, step_count, action_width)
    keep_dims = (jnp.arange(action_width)[None, :] < action_dims[:, None]).astype(jnp.float32)
    mismatch = (predicted - (flow_noise - action_stretch)) * keep_dims[:, None, :]
    loss_local = jnp.sum(mismatch * mismatch)

    grad_pred = (2.0 * mismatch / counted).reshape(row_count, -1).astype(low_precision)
    grad_head = product(head_in.T, grad_pred)
    grad_top, gain_grad_three = norm_backward(
        product(grad_pred, out_proj.T), unit_three, inverse_three, gain_three
    )
    grad_mlp = grad_top.astype(low_precision)
    grad_mlp_all = share_rows(grad_mlp)
    grad_down = product(hidden.T, grad_mlp_all).astype(low_precision)
    grad_hidden = product(grad_mlp_all, down_proj.T)
    glu_value, glu_pull = jax.vjp(glu_unit, gate_part, up_part)
    grad_gate_up = jnp.concatenate(glu_pull(grad_hidden), axis=1).astype(low_precision)
    grad_mlp_in = return_rows(product(grad_gate_up, gate_up_proj.T))
    grad_sides = product(mlp_all.T, grad_gate_up).astype(low_precision)
    grad_layer = jnp.concatenate([grad_sides, grad_down.reshape(inner_width, -1)], axis=1)
    grad_mlp_in = after(grad_mlp_in, grad_layer)
    grad_layer = lax.psum_scatter(grad_layer, "wide", scatter_dimension=0, tiled=True)
    grad_gate_up = swap_out(grad_sides, unit_groups)
    grad_mlp_in, gain_grad_two = norm_backward(grad_mlp_in, unit_two, inverse_two, gain_two)
    grad_mid = grad_top + grad_mlp_in
    grad_branch = grad_mid.astype(low_precision)
    grad_out_att = product(attended.T, grad_branch).astype(low_precision)
    grad_out_att = core_sum(grad_out_att.reshape((devices,) + attn_out.shape))
    out_send, out_keep = part_ways(grad_out_att, near_bit(), 1)
    grad_attended = after(product(grad_branch, out_att.T).astype(low_precision), out_send)
    grad_attended = grad_attended.reshape(item_rows)
    grad_queries, grad_own, *spread = attend_back(
        pieces,
        offsets,
        mine_start,
        mine_end,
        queries,
        own_kv,
        grad_attended,
        attended_rows,
        lse,
        step_count,
        stream_len,
    )
    if narrow:
        core_part = flip(spread[1], CORE)
        inner_part = trade_list(spread[2], [(1, 2), (2, 1)])
        tail_part = trade_list(spread[3], [(1, 3), (2, 0)])
        blank = jnp.zeros_like(tail_part)
        reached = (inner_part, core_part, tail_part)
        grad_prefix = (
            spread[0]
            + core_part
            + inner_part
            + jnp.pad(jnp.where(act_rank == 3, tail_part, blank), ((0, chunk - tail), (0, 0)))
            + jnp.pad(jnp.where(act_rank == 0, tail_part, blank), ((chunk - tail, 0), (0, 0)))
        )
    else:
        for bit in [CORE] + row_bits()[::-1]:
            half = len(spread) // 2
            spread = [
                piece + flip(other, bit) for piece, other in zip(spread[:half], spread[half:])
            ]
        grad_prefix = spread[0]
        reached = (grad_prefix,)
    grad_projected = jnp.concatenate(
        [
            grad_queries.reshape(row_count, query_width),
            grad_own[:, :step_count].reshape(row_count, 2 * head_size),
        ],
        axis=1,
    )
    grad_projected = after(grad_projected, *reached[1:])
    grad_qkv = product(attn_in.T, grad_projected).astype(low_precision)
    grad_attn_in, gain_grad_one = norm_backward(
        product(grad_projected, qkv_proj.T), unit_one, inverse_one, gain_one
    )
    grad_base = (grad_mid + grad_attn_in).astype(low_precision)
    grad_in = product(features.T, grad_base)
    grad_qkv = core_sum(grad_qkv.reshape((devices,) + action_qkv.shape))
    qkv_send, qkv_keep = part_ways(grad_qkv, near_bit(), 1)
    grad_out_att = meet(out_send, out_keep, near_bit(), qkv_send, *reached)
    grad_prefix = after(grad_prefix, grad_out_att)
    grad_kv = product(pre_in.T, grad_prefix)
    gain_grad_pre = jnp.sum(grad_kv * kv_proj.astype(jnp.float32), axis=1) / gain_pre
    grad_gains = jnp.concatenate([gain_grad_pre, gain_grad_one, gain_grad_two, gain_grad_three])
    small_grads = [
        part.astype(low_precision).reshape((devices,) + shard.shape)
        for part, shard in zip((grad_kv, grad_in, grad_head, grad_gains), small_shards)
    ]
    small_grads = pack_rows(small_grads, pack_width)
    far = 2 ** len(far_bits())
    small_core = halve(small_grads.reshape((-1, 2) + small_grads.shape[1:]), CORE, 1)
    small_core = small_core.reshape((far, -1) + small_core.shape[1:]).swapaxes(0, 1)
    small_core = after(small_core, grad_layer)
    grad_qkv = meet(qkv_send, qkv_keep, near_bit(), small_core)
    for bit in row_bits():
        grad_out_att = halve(grad_out_att, bit, 1, small_core)
    small_plane = hand_out(small_core, [near_bit()] + row_bits()).astype(low_precision)
    grad_layer = after(grad_layer, small_core)
    grad_down = grad_layer[:, side_width:].reshape(action_down.shape)
    grad_gate_up = swap_out(grad_layer[:, :side_width], unit_groups)
    grad_out_att = hand_out(grad_out_att, far_bits(), small_plane)
    small_grads = hand_out(small_plane, far_bits())
    for bit in row_bits():
        grad_qkv = halve(grad_qkv, bit, 1, small_plane)
    grad_qkv = hand_out(grad_qkv, far_bits(), small_grads)
    small_grads = unpack_rows(small_grads[None], small_shapes)
    grad_kv, grad_in, grad_head, grad_gains = (part[0] for part in small_grads)
    gradients = (
        grad_gains,
        grad_kv,
        grad_in,
        grad_qkv,
        grad_out_att,
        grad_gate_up.astype(jnp.float32),
        grad_down.astype(jnp.float32),
        grad_head,
    )
    local_squares = sum((jnp.sum(grad_one * grad_one) for grad_one in gradients))
    sums = total(jnp.stack([loss_local, local_squares]))
    loss_sum = sums[0]
    grad_norm = jnp.sqrt(sums[1])
    clip_factor = jnp.minimum(1.0, CLIP_AT / (grad_norm + 1e-06))
    step_rates = (GAIN_RATE,) + (MATRIX_RATE,) * 7
    decay_rates = (0.0,) + (WEIGHT_DECAY,) * 7
    updated = []
    for master_w, moment_one, moment_two, gradient, step_rate, decay_rate in zip(
        masters, moments_one, moments_two, gradients, step_rates, decay_rates
    ):
        updated.extend(
            adamw(master_w, moment_one, moment_two, gradient * clip_factor, step_rate, decay_rate)
        )
    return (
        updated[0],
        updated[1],
        updated[2],
        updated[3],
        updated[4],
        updated[5],
        updated[6],
        updated[7],
        updated[8],
        updated[9],
        updated[10],
        updated[11],
        updated[12],
        updated[13],
        updated[14],
        updated[15],
        updated[16],
        updated[17],
        updated[18],
        updated[19],
        updated[20],
        updated[21],
        updated[22],
        updated[23],
        loss_sum,
        counted,
        grad_norm,
    )


def solution(mesh):
    wide, act = mesh.devices.shape
    lanes_mesh = Mesh(mesh.devices.reshape(wide, act // 2, 2), AXES)
    placed = (
        P(AXES, None),
        P("wide", None),
        P(AXES, None, None),
        P(AXES, None, None),
        P(AXES),
        P(AXES),
        P(AXES),
        P(AXES),
        P(AXES),
        P(AXES, None),
        P(AXES, None),
        P(AXES, None),
        P(AXES, None),
        P(AXES, None),
        P(AXES, None),
        P(AXES, None),
        P(AXES, None),
        P(AXES, None),
        P(AXES, None),
        P(AXES, None),
        P(AXES, None),
        P(AXES, None),
        P(AXES, None),
        P(AXES, None),
        P(AXES, None),
        P(AXES, None),
        P(AXES, None),
        P(AXES, None),
        P(AXES, None),
        P(AXES, None),
    )
    return jax.shard_map(
        on_device,
        mesh=lanes_mesh,
        in_specs=placed,
        out_specs=(
            P(AXES),
            P(AXES),
            P(AXES),
            P(AXES, None),
            P(AXES, None),
            P(AXES, None),
            P(AXES, None),
            P(AXES, None),
            P(AXES, None),
            P(AXES, None),
            P(AXES, None),
            P(AXES, None),
            P(AXES, None),
            P(AXES, None),
            P(AXES, None),
            P(AXES, None),
            P(AXES, None),
            P(AXES, None),
            P(AXES, None),
            P(AXES, None),
            P(AXES, None),
            P(AXES, None),
            P(AXES, None),
            P(AXES, None),
            P(),
            P(),
            P(),
        ),
        check_vma=False,
    )
```

```python
import functools

import jax
import jax.numpy as jnp
from jax import lax
from jax.experimental import pallas as pl
from jax.experimental.pallas import tpu as pltpu
from jax.sharding import Mesh
from jax.sharding import PartitionSpec as P

TFEAT = 96
PMAX = 1024
STEP = 10
KERNEL_BYTES = 48 * 1024 * 1024


NORM_EPS = 1e-06
CLIP_AT = 0.005
BETA_ONE = 0.9
BETA_TWO = 0.95
ADAM_EPS = 1e-08
MATRIX_RATE = 0.02
GAIN_RATE = 0.7
WEIGHT_DECAY = 0.01


def product(matrix_a, matrix_b):
    return jnp.dot(matrix_a, matrix_b, preferred_element_type=jnp.float32)


def norm_forward(values, scaling):
    inverse = lax.rsqrt(jnp.mean(values * values, axis=-1, keepdims=True) + NORM_EPS)
    unit_vals = values * inverse
    return (unit_vals * scaling, unit_vals, inverse)


def norm_backward(grad_out, unit_vals, inverse, scaling):
    grad_unit = grad_out * scaling
    grad_in = inverse * (
        grad_unit - unit_vals * jnp.mean(grad_unit * unit_vals, axis=-1, keepdims=True)
    )
    return (grad_in, jnp.sum(grad_out * unit_vals, axis=0))


def time_features(stamps, feat_width):
    half_width = feat_width // 2
    ladder = jnp.arange(half_width, dtype=jnp.float32) / (half_width - 1)
    frequency = 6.283185307179586 / (0.004 * 1000.0**ladder)
    angles = stamps[:, None] * frequency[None, :]
    return jnp.concatenate([jnp.sin(angles), jnp.cos(angles)], axis=1)


def glu_unit(gate_in, up_in):
    return jax.nn.gelu(gate_in, approximate=True) * up_in


def adamw(master_w, moment_one, moment_two, gradient, step_rate, decay_rate):
    first_new = BETA_ONE * moment_one + (1.0 - BETA_ONE) * gradient
    second_new = BETA_TWO * moment_two + (1.0 - BETA_TWO) * gradient * gradient
    first_hat = first_new / (1.0 - BETA_ONE**STEP)
    second_hat = second_new / (1.0 - BETA_TWO**STEP)
    master_new = master_w - step_rate * (
        first_hat / (jnp.sqrt(second_hat) + ADAM_EPS) + decay_rate * master_w
    )
    return (master_new, first_new, second_new)


def split_gains(gains_all, model_width, inner_width):
    gains_f = gains_all.astype(jnp.float32)
    return (
        gains_f[:model_width],
        gains_f[model_width : model_width + inner_width],
        gains_f[model_width + inner_width : model_width + 2 * inner_width],
        gains_f[model_width + 2 * inner_width :],
    )


AXES = ("wide", "row", "core")
CORE = 1


def device_count():
    return lax.axis_size(AXES)


def act_count():
    return lax.axis_size(("row", "core"))


def flip(block, mask):
    return lax.ppermute(block, AXES, [(place, place ^ mask) for place in range(device_count())])


def my_bit(mask):
    return (lax.axis_index(AXES) // mask) % 2


def bits_between(low, high):
    bits = []
    while low < high:
        bits.append(low)
        low *= 2
    return bits[::-1]


def row_bits():
    return bits_between(2, act_count())


def near_bit():
    return act_count()


def far_bits():
    return bits_between(2 * act_count(), device_count())


def combos(bits):
    masks = [0]
    for bit in bits:
        masks = [mask + more for mask in masks for more in (0, bit)]
    return masks


def settle(blocks, bits):
    for number, bit in enumerate(bits):
        step = len(blocks) >> (number + 1)
        swap = my_bit(bit) == 1
        blocks = [jnp.where(swap, blocks[at ^ step], blocks[at]) for at in range(len(blocks))]
    return blocks


def after(block, *others):
    return lax.optimization_barrier((block,) + others)[0]


def fetch(block, bits, *others):
    blocks = [block if mask == 0 else flip(block, mask) for mask in combos(bits)]
    if others:
        blocks = lax.optimization_barrier((blocks,) + others)[0]
    return jnp.stack(settle(blocks, bits))


def double(block, bit, at, *others):
    other = flip(block, bit)
    if others:
        other = after(other, *others)
    return jnp.stack(settle([block, other], [bit]), axis=at)


def place_index(bits):
    index = 0
    for bit in bits:
        index = 2 * index + my_bit(bit)
    return index


def pick(block, index, at):
    return lax.dynamic_index_in_dim(block, index, at, keepdims=False)


def wide_sum(blocks):
    return sum(block.astype(jnp.float32) for block in blocks)


def part_ways(block, bit, at):
    mine = my_bit(bit)
    return pick(block, 1 - mine, at), pick(block, mine, at)


def meet(send, keep, bit, *others):
    other = flip(send, bit)
    if others:
        other = after(other, *others)
    return wide_sum([keep, other]).astype(jnp.bfloat16)


def halve(block, bit, at, *others):
    return meet(*part_ways(block, bit, at), bit, *others)


def hand_out(block, bits, *others):
    mine = place_index(bits)
    blocks = [pick(block, mine, 0)]
    for number, mask in enumerate(combos(bits)):
        if mask:
            blocks.append(flip(pick(block, mine ^ number, 0), mask))
    if others:
        blocks = lax.optimization_barrier((blocks,) + others)[0]
    return wide_sum(blocks)


def core_sum(block):
    rows, columns = block.shape[1:]
    far = 2 ** len(far_bits())
    block = halve(block.reshape(-1, 2, rows, columns), CORE, 1)
    return block.reshape((far, 2) + (2,) * len(row_bits()) + (rows, columns))


def row_sum(block):
    for bit in row_bits():
        block = halve(block, bit, 2)
    return block


def total(value):
    for bit in bits_between(1, device_count())[::-1]:
        value = value + flip(value, bit)
    return value


def trade_list(block, pairs):
    group = act_count()
    return lax.ppermute(
        block,
        AXES,
        [
            (start + sender, start + receiver)
            for start in range(0, device_count(), group)
            for sender, receiver in pairs
        ],
    )


def share_rows(block):
    for bit in row_bits() + [CORE]:
        block = jnp.concatenate([block, flip(block, bit)])
    return block


def return_rows(block):
    for bit in [CORE] + row_bits()[::-1]:
        half = block.shape[0] // 2
        other = flip(block[half:].astype(jnp.bfloat16), bit)
        block = block[:half] + other.astype(jnp.float32)
    return block


def swap_in(block):
    rows, groups, size, unit = block.shape
    bits = row_bits() + [CORE]
    block = block.reshape((rows, groups) + (2,) * len(bits) + (unit,))
    for done, bit in enumerate(bits):
        mine = my_bit(bit)
        other = flip(pick(block, 1 - mine, done + 2), bit)
        block = jnp.stack(settle([pick(block, mine, done + 2), other], [bit]), axis=done)
    return block.reshape(size * rows, groups * unit)


def swap_out(block, groups):
    bits = row_bits() + [CORE]
    size = act_count()
    rows, unit = block.shape[0] // size, block.shape[1] // groups
    block = block.reshape((2,) * len(bits) + (rows, groups, unit))
    for left in range(len(bits) - 1, -1, -1):
        mine = my_bit(bits[left])
        other = flip(pick(block, 1 - mine, left), bits[left])
        block = jnp.stack(settle([pick(block, mine, left), other], [bits[left]]), axis=left + 2)
    return block.reshape(rows, groups * size * unit)


def pack_rows(parts, width):
    lead = parts[0].shape[0]
    rows = []
    for part in parts:
        flat = part.reshape(lead, -1)
        short = -flat.shape[1] % width
        rows.append(jnp.pad(flat, ((0, 0), (0, short))).reshape(lead, -1, width))
    packed = jnp.concatenate(rows, axis=1)
    return jnp.pad(packed, ((0, 0), (0, -packed.shape[1] % 16), (0, 0)))


def unpack_rows(packed, shapes):
    lead, width = packed.shape[0], packed.shape[2]
    parts, at = [], 0
    for shape in shapes:
        size = 1
        for extent in shape:
            size *= extent
        count = -(-size // width)
        flat = packed[:, at : at + count].reshape(lead, -1)[:, :size]
        parts.append(flat.reshape((lead,) + tuple(shape)))
        at += count
    return parts


KEY_BLOCK = 512


def span(first, last, at):
    begin = first[at] // 16 * 16
    return begin, (last[at] - begin + KEY_BLOCK - 1) // KEY_BLOCK


def load_stream(piece_refs, offsets, stream, sems):
    count = len(piece_refs)
    for number in range(count, offsets.shape[0]):
        row = pl.multiple_of(offsets[number], 16)
        stream[pl.ds(row, KEY_BLOCK), :] = jnp.zeros((KEY_BLOCK, stream.shape[1]), stream.dtype)
    copies = []
    for number, piece in enumerate(piece_refs):
        row = pl.multiple_of(offsets[number], 16)
        copies.append(
            pltpu.make_async_copy(
                piece, stream.at[pl.ds(row, piece.shape[0]), :], sems.at[number]
            )
        )
    for copy in copies:
        copy.start()
    for copy in copies:
        copy.wait()


def across(matrix_a, matrix_b):
    return lax.dot_general(
        matrix_a, matrix_b, (((1,), (1,)), ((), ())), preferred_element_type=jnp.float32
    )


def down_rows(matrix_a, matrix_b):
    return lax.dot_general(
        matrix_a, matrix_b, (((0,), (0,)), ((), ())), preferred_element_type=jnp.float32
    )


def attend_kernel(piece_count, step_count, first, last, offsets, query_ref, own_ref, *refs):
    piece_refs = refs[:piece_count]
    out_ref, lse_ref, stream, sems = refs[piece_count:]
    head_size = query_ref.shape[2]
    scale = head_size ** (-0.5)
    load_stream(piece_refs, offsets, stream, sems)

    def item(at, carry):
        query = query_ref[at]
        own = own_ref[at]
        scores = across(query, own[:, :head_size]) * scale
        column = lax.broadcasted_iota(jnp.int32, (1, own.shape[0]), 1)
        scores = jnp.where(column < step_count, scores, -1e30)
        top = jnp.max(scores, axis=1, keepdims=True)
        probs = jnp.exp(scores - top)
        mass = jnp.sum(probs, axis=1, keepdims=True)
        held = product(probs.astype(jnp.bfloat16), own[:, head_size:])
        begin, blocks = span(first, last, at)

        def block(number, state):
            top, mass, held = state
            row = pl.multiple_of(begin + number * KEY_BLOCK, 16)
            pairs = stream[pl.ds(row, KEY_BLOCK), :]
            scores = across(query, pairs[:, :head_size]) * scale
            place = row + lax.broadcasted_iota(jnp.int32, (1, KEY_BLOCK), 1)
            live = (place >= first[at]) & (place < last[at])
            scores = jnp.where(live, scores, -1e30)
            top_new = jnp.maximum(top, jnp.max(scores, axis=1, keepdims=True))
            shrink = jnp.exp(top - top_new)
            probs = jnp.exp(scores - top_new)
            mass = mass * shrink + jnp.sum(probs, axis=1, keepdims=True)
            held = held * shrink + product(probs.astype(jnp.bfloat16), pairs[:, head_size:])
            return top_new, mass, held

        top, mass, held = lax.fori_loop(0, blocks, block, (top, mass, held))
        out_ref[at] = (held / mass).astype(out_ref.dtype)
        lse_ref[at] = top + jnp.log(mass)
        return carry

    lax.fori_loop(0, query_ref.shape[0], item, 0)


def attend(pieces, offsets, first, last, queries, own, step_count, stream_len):
    items, rows, head_size = queries.shape
    stream_rows = stream_len + KEY_BLOCK
    scalars = pl.BlockSpec(memory_space=pltpu.SMEM)
    whole = pl.BlockSpec(memory_space=pltpu.VMEM)
    far = pl.BlockSpec(memory_space=pl.ANY)
    return pl.pallas_call(
        functools.partial(attend_kernel, len(pieces), step_count),
        out_shape=(
            jax.ShapeDtypeStruct(queries.shape, jnp.bfloat16),
            jax.ShapeDtypeStruct((items, rows, 1), jnp.float32),
        ),
        in_specs=[scalars] * 3 + [whole] * 2 + [far] * len(pieces),
        out_specs=(whole, whole),
        scratch_shapes=[
            pltpu.VMEM((stream_rows, 2 * head_size), jnp.bfloat16),
            pltpu.SemaphoreType.DMA((len(pieces),)),
        ],
        compiler_params=pltpu.CompilerParams(vmem_limit_bytes=KERNEL_BYTES),
        cost_estimate=pl.CostEstimate(flops=1, bytes_accessed=1, transcendentals=0),
        name="attend",
    )(first, last, offsets, queries, own, *pieces)


def attend_back_kernel(piece_count, step_count, first, last, offsets, *refs):
    query_ref, own_ref, grad_ref, out_ref, lse_ref = refs[:5]
    piece_refs = refs[5 : 5 + piece_count]
    grad_query_ref, grad_own_ref = refs[5 + piece_count : 7 + piece_count]
    spread_refs = refs[7 + piece_count : 7 + 2 * piece_count]
    stream, spread, sems = refs[7 + 2 * piece_count :]
    head_size = query_ref.shape[2]
    scale = head_size ** (-0.5)

    def clear(number, carry):
        row = pl.multiple_of(number * KEY_BLOCK, KEY_BLOCK)
        spread[pl.ds(row, KEY_BLOCK), :] = jnp.zeros((KEY_BLOCK, spread.shape[1]), spread.dtype)
        return carry

    lax.fori_loop(0, spread.shape[0] // KEY_BLOCK, clear, 0)
    load_stream(piece_refs, offsets, stream, sems)

    def item(at, carry):
        query = query_ref[at]
        grad = grad_ref[at]
        lse = lse_ref[at]
        mean = jnp.sum(
            grad.astype(jnp.float32) * out_ref[at].astype(jnp.float32), axis=1, keepdims=True
        )

        def pull(pairs, live):
            keys = pairs[:, :head_size]
            scores = across(query, keys) * scale
            probs = jnp.where(live, jnp.exp(scores - lse), 0.0)
            grad_probs = across(grad, pairs[:, head_size:])
            grad_scores = (probs * (grad_probs - mean)).astype(jnp.bfloat16)
            grad_values = down_rows(probs.astype(jnp.bfloat16), grad)
            grad_keys = down_rows(grad_scores, query) * scale
            return (
                product(grad_scores, keys),
                grad_keys.astype(jnp.bfloat16),
                grad_values.astype(jnp.bfloat16),
            )

        own = own_ref[at]
        column = lax.broadcasted_iota(jnp.int32, (1, own.shape[0]), 1)
        grad_query, grad_keys, grad_values = pull(own, column < step_count)
        grad_own_ref[at, :, :head_size] = grad_keys
        grad_own_ref[at, :, head_size:] = grad_values
        begin, blocks = span(first, last, at)

        def block(number, grad_query):
            row = pl.multiple_of(begin + number * KEY_BLOCK, 16)
            place = row + lax.broadcasted_iota(jnp.int32, (1, KEY_BLOCK), 1)
            live = (place >= first[at]) & (place < last[at])
            more, grad_keys, grad_values = pull(stream[pl.ds(row, KEY_BLOCK), :], live)
            spread[pl.ds(row, KEY_BLOCK), :head_size] += grad_keys
            spread[pl.ds(row, KEY_BLOCK), head_size:] += grad_values
            return grad_query + more

        grad_query = lax.fori_loop(0, blocks, block, grad_query)
        grad_query_ref[at] = (grad_query * scale).astype(grad_query_ref.dtype)
        return carry

    lax.fori_loop(0, query_ref.shape[0], item, 0)
    copies = []
    for number, piece in enumerate(spread_refs):
        row = pl.multiple_of(offsets[number], 16)
        copies.append(
            pltpu.make_async_copy(
                spread.at[pl.ds(row, piece.shape[0]), :], piece, sems.at[number]
            )
        )
    for copy in copies:
        copy.start()
    for copy in copies:
        copy.wait()


def attend_back(pieces, offsets, first, last, queries, own, grad, out, lse, step_count, stream_len):
    items, rows, head_size = queries.shape
    stream_rows = stream_len + KEY_BLOCK
    scalars = pl.BlockSpec(memory_space=pltpu.SMEM)
    whole = pl.BlockSpec(memory_space=pltpu.VMEM)
    far = pl.BlockSpec(memory_space=pl.ANY)
    return pl.pallas_call(
        functools.partial(attend_back_kernel, len(pieces), step_count),
        out_shape=(
            jax.ShapeDtypeStruct(queries.shape, jnp.bfloat16),
            jax.ShapeDtypeStruct(own.shape, jnp.bfloat16),
        )
        + tuple(jax.ShapeDtypeStruct(piece.shape, jnp.bfloat16) for piece in pieces),
        in_specs=[scalars] * 3 + [whole] * 5 + [far] * len(pieces),
        out_specs=(whole, whole) + (far,) * len(pieces),
        scratch_shapes=[
            pltpu.VMEM((stream_rows, 2 * head_size), jnp.bfloat16),
            pltpu.VMEM((stream_rows, 2 * head_size), jnp.bfloat16),
            pltpu.SemaphoreType.DMA((len(pieces),)),
        ],
        compiler_params=pltpu.CompilerParams(vmem_limit_bytes=KERNEL_BYTES),
        cost_estimate=pl.CostEstimate(flops=1, bytes_accessed=1, transcendentals=0),
        name="attend_back",
    )(first, last, offsets, queries, own, grad, out, lse, *pieces)


def on_device(
    prefix_rows,
    item_lengths,
    action_stretch,
    flow_noise,
    flow_times,
    action_dims,
    norm_gains,
    norm_gains_first,
    norm_gains_second,
    prefix_kv,
    prefix_kv_first,
    prefix_kv_second,
    action_in,
    action_in_first,
    action_in_second,
    action_qkv,
    action_qkv_first,
    action_qkv_second,
    attn_out,
    attn_out_first,
    attn_out_second,
    action_gate_up,
    action_gate_up_first,
    action_gate_up_second,
    action_down,
    action_down_first,
    action_down_second,
    action_head,
    action_head_first,
    action_head_second,
):
    masters = (
        norm_gains,
        prefix_kv,
        action_in,
        action_qkv,
        attn_out,
        action_gate_up,
        action_down,
        action_head,
    )
    moments_one = (
        norm_gains_first,
        prefix_kv_first,
        action_in_first,
        action_qkv_first,
        attn_out_first,
        action_gate_up_first,
        action_down_first,
        action_head_first,
    )
    moments_two = (
        norm_gains_second,
        prefix_kv_second,
        action_in_second,
        action_qkv_second,
        attn_out_second,
        action_gate_up_second,
        action_down_second,
        action_head_second,
    )
    inner_width = action_down.shape[1]
    devices = device_count()
    group = act_count()
    low_precision = jnp.bfloat16

    dims_sum = jnp.sum(action_dims).astype(jnp.float32).reshape(1, 1)
    small_shards = (prefix_kv, action_in, action_head, norm_gains)
    small_shapes = [part.shape for part in small_shards]
    pack_width = prefix_kv.shape[1]
    small = pack_rows(
        [part.astype(low_precision)[None] for part in small_shards + (dims_sum,)], pack_width
    )[0]
    small_far = fetch(small, far_bits())
    small = fetch(small_far, [near_bit()] + row_bits()).swapaxes(0, 1)
    small = double(small, CORE, 2)
    small_all = unpack_rows(
        small.reshape((devices,) + small.shape[-2:]), small_shapes + [(1, 1)]
    )
    kv_proj, in_proj, out_proj, gains_all = (
        part.reshape((-1,) + part.shape[2:]) for part in small_all[:4]
    )
    counted = jnp.float32(action_stretch.shape[1]) * jnp.sum(small_all[4].astype(jnp.float32))

    hidden_width = action_gate_up.shape[1] // 2
    unit_block = action_down.shape[0]
    unit_groups = 2 * hidden_width // (group * unit_block)
    side_width = unit_groups * unit_block
    sides = swap_in(
        action_gate_up.astype(low_precision).reshape(-1, unit_groups, group, unit_block)
    )
    side_rows = sides.shape[0]
    qkv_proj = lax.all_gather(action_qkv.astype(low_precision), AXES, axis=0, tiled=True)
    layer = jnp.concatenate(
        [sides, action_down.astype(low_precision).reshape(side_rows, -1)], axis=1
    )
    layer = lax.all_gather(layer, "wide", axis=0, tiled=True)
    gate_up_proj = layer[:, :side_width]
    down_proj = layer[:, side_width:].reshape(side_width // 2, inner_width)

    model_width = prefix_rows.shape[1]
    query_width = devices * attn_out.shape[0]
    head_size = (action_qkv.shape[1] - query_width) // 2
    head_count = query_width // head_size
    item_count, step_count, action_width = action_stretch.shape
    row_count = item_count * step_count
    gain_pre, gain_one, gain_two, gain_three = split_gains(gains_all, model_width, inner_width)
    pre_normed, pre_unit, pre_inverse = norm_forward(prefix_rows.astype(jnp.float32), gain_pre)
    pre_in = pre_normed.astype(low_precision)
    pre_keys = product(pre_in, kv_proj).astype(low_precision)
    act_rank = lax.axis_index(("row", "core"))
    chunk = pre_keys.shape[0]
    stream_len = group * chunk
    reach = action_stretch.shape[0] * PMAX
    tail = 2 * reach - 3 * chunk
    narrow = group == 4 and reach <= 2 * chunk and 0 < tail <= chunk and tail % 16 == 0
    if narrow:
        outer_end = jnp.where(act_rank == 0, pre_keys[chunk - tail :], pre_keys[:tail])
        pieces = [
            pre_keys,
            flip(pre_keys, CORE),
            trade_list(pre_keys, [(1, 2), (2, 1)]),
            trade_list(outer_end, [(3, 1), (0, 2)]),
        ]
        tail_at = pick(jnp.array([2 * chunk, 3 * chunk, chunk - tail, chunk]), act_rank, 0)
        offsets = jnp.stack(
            [
                act_rank * chunk,
                (act_rank ^ 1) * chunk,
                (3 - act_rank) * chunk,
                tail_at,
                jnp.full_like(tail_at, stream_len),
                jnp.full_like(tail_at, 3 * chunk + tail),
            ]
        )
    else:
        pieces = [pre_keys]
        ranks = [0]
        for bit in row_bits() + [CORE]:
            pieces += [flip(piece, bit) for piece in pieces]
            ranks += [rank + bit for rank in ranks]
        offsets = jnp.stack(
            [(act_rank ^ rank) * chunk for rank in ranks]
            + [jnp.full_like(act_rank, stream_len)]
        )

    ends_at = jnp.cumsum(item_lengths[0])
    mine_end = lax.dynamic_slice_in_dim(ends_at, act_rank * item_count, item_count)
    mine_start = lax.dynamic_slice_in_dim(
        ends_at - item_lengths[0], act_rank * item_count, item_count
    )
    blend_t = flow_times[:, None, None]
    noisy_acts = blend_t * flow_noise + (1.0 - blend_t) * action_stretch
    stamp_feats = jnp.broadcast_to(
        time_features(flow_times, TFEAT)[:, None, :], (item_count, step_count, TFEAT)
    )
    features = (
        jnp.concatenate([noisy_acts, stamp_feats], axis=2)
        .reshape(row_count, -1)
        .astype(low_precision)
    )
    base_res = product(features, in_proj)
    attn_normed, unit_one, inverse_one = norm_forward(base_res, gain_one)
    attn_in = attn_normed.astype(low_precision)
    projected = product(attn_in, qkv_proj)
    item_rows = (item_count, step_count * head_count, head_size)
    queries = projected[:, :query_width].astype(low_precision).reshape(item_rows)
    own_kv = (
        projected[:, query_width:]
        .astype(low_precision)
        .reshape(item_count, step_count, 2 * head_size)
    )
    own_kv = jnp.pad(own_kv, ((0, 0), (0, -step_count % 64), (0, 0)))
    out_att = fetch(after(attn_out.astype(low_precision), small), far_bits(), queries)
    out_att = after(double(out_att, near_bit(), 1), *pieces)
    attended_rows, lse = attend(
        pieces, offsets, mine_start, mine_end, after(queries, out_att), own_kv, step_count, stream_len
    )
    for bit in row_bits() + [CORE]:
        out_att = double(out_att, bit, -3, attended_rows)
    out_att = out_att.reshape(query_width, inner_width)
    attended = attended_rows.reshape(row_count, query_width)
    mid_res = base_res + product(attended, out_att)
    mlp_normed, unit_two, inverse_two = norm_forward(mid_res, gain_two)
    mlp_in = mlp_normed.astype(low_precision)
    mlp_all = share_rows(mlp_in)
    gate_vals = product(mlp_all, gate_up_proj)
    half_side = side_width // 2
    gate_part, up_part = gate_vals[:, :half_side], gate_vals[:, half_side:]
    hidden = glu_unit(gate_part, up_part).astype(low_precision)
    top_res = mid_res + return_rows(product(hidden, down_proj))
    head_normed, unit_three, inverse_three = norm_forward(top_res, gain_three)
    head_in = head_normed.astype(low_precision)
    predicted = product(head_in, out_proj).reshape(item_count, step_count, action_width)
    keep_dims = (jnp.arange(action_width)[None, :] < action_dims[:, None]).astype(jnp.float32)
    mismatch = (predicted - (flow_noise - action_stretch)) * keep_dims[:, None, :]
    loss_local = jnp.sum(mismatch * mismatch)

    grad_pred = (2.0 * mismatch / counted).reshape(row_count, -1).astype(low_precision)
    grad_head = product(head_in.T, grad_pred)
    grad_top, gain_grad_three = norm_backward(
        product(grad_pred, out_proj.T), unit_three, inverse_three, gain_three
    )
    grad_mlp = grad_top.astype(low_precision)
    grad_mlp_all = share_rows(grad_mlp)
    grad_down = product(hidden.T, grad_mlp_all).astype(low_precision)
    grad_hidden = product(grad_mlp_all, down_proj.T)
    glu_value, glu_pull = jax.vjp(glu_unit, gate_part, up_part)
    grad_gate_up = jnp.concatenate(glu_pull(grad_hidden), axis=1).astype(low_precision)
    grad_mlp_in = return_rows(product(grad_gate_up, gate_up_proj.T))
    grad_sides = product(mlp_all.T, grad_gate_up).astype(low_precision)
    grad_layer = jnp.concatenate([grad_sides, grad_down.reshape(inner_width, -1)], axis=1)
    grad_mlp_in = after(grad_mlp_in, grad_layer)
    grad_layer = lax.psum_scatter(grad_layer, "wide", scatter_dimension=0, tiled=True)
    grad_gate_up = swap_out(grad_sides, unit_groups)
    grad_mlp_in, gain_grad_two = norm_backward(grad_mlp_in, unit_two, inverse_two, gain_two)
    grad_mid = grad_top + grad_mlp_in
    grad_branch = grad_mid.astype(low_precision)
    grad_out_att = product(attended.T, grad_branch).astype(low_precision)
    grad_out_att = core_sum(grad_out_att.reshape((devices,) + attn_out.shape))
    out_send, out_keep = part_ways(grad_out_att, near_bit(), 1)
    grad_attended = after(product(grad_branch, out_att.T).astype(low_precision), out_send)
    grad_attended = grad_attended.reshape(item_rows)
    grad_queries, grad_own, *spread = attend_back(
        pieces,
        offsets,
        mine_start,
        mine_end,
        queries,
        own_kv,
        grad_attended,
        attended_rows,
        lse,
        step_count,
        stream_len,
    )
    if narrow:
        core_part = flip(spread[1], CORE)
        inner_part = trade_list(spread[2], [(1, 2), (2, 1)])
        tail_part = trade_list(spread[3], [(1, 3), (2, 0)])
        blank = jnp.zeros_like(tail_part)
        reached = (inner_part, core_part, tail_part)
        grad_prefix = (
            spread[0]
            + core_part
            + inner_part
            + jnp.pad(jnp.where(act_rank == 3, tail_part, blank), ((0, chunk - tail), (0, 0)))
            + jnp.pad(jnp.where(act_rank == 0, tail_part, blank), ((chunk - tail, 0), (0, 0)))
        )
    else:
        for bit in [CORE] + row_bits()[::-1]:
            half = len(spread) // 2
            spread = [
                piece + flip(other, bit) for piece, other in zip(spread[:half], spread[half:])
            ]
        grad_prefix = spread[0]
        reached = (grad_prefix,)
    grad_projected = jnp.concatenate(
        [
            grad_queries.reshape(row_count, query_width),
            grad_own[:, :step_count].reshape(row_count, 2 * head_size),
        ],
        axis=1,
    )
    grad_projected = after(grad_projected, *reached[1:])
    grad_qkv = product(attn_in.T, grad_projected).astype(low_precision)
    grad_attn_in, gain_grad_one = norm_backward(
        product(grad_projected, qkv_proj.T), unit_one, inverse_one, gain_one
    )
    grad_base = (grad_mid + grad_attn_in).astype(low_precision)
    grad_in = product(features.T, grad_base)
    grad_qkv = core_sum(grad_qkv.reshape((devices,) + action_qkv.shape))
    qkv_send, qkv_keep = part_ways(grad_qkv, near_bit(), 1)
    grad_out_att = meet(out_send, out_keep, near_bit(), qkv_send, *reached)
    grad_prefix = after(grad_prefix, grad_out_att)
    grad_kv = product(pre_in.T, grad_prefix)
    gain_grad_pre = jnp.sum(grad_kv * kv_proj.astype(jnp.float32), axis=1) / gain_pre
    grad_gains = jnp.concatenate([gain_grad_pre, gain_grad_one, gain_grad_two, gain_grad_three])
    small_grads = [
        part.astype(low_precision).reshape((devices,) + shard.shape)
        for part, shard in zip((grad_kv, grad_in, grad_head, grad_gains), small_shards)
    ]
    small_grads = pack_rows(small_grads, pack_width)
    far = 2 ** len(far_bits())
    small_core = halve(small_grads.reshape((-1, 2) + small_grads.shape[1:]), CORE, 1)
    small_core = small_core.reshape((far, -1) + small_core.shape[1:]).swapaxes(0, 1)
    small_core = after(small_core, grad_layer)
    grad_qkv = meet(qkv_send, qkv_keep, near_bit(), small_core)
    for bit in row_bits():
        grad_out_att = halve(grad_out_att, bit, 1, small_core)
    small_plane = hand_out(small_core, [near_bit()] + row_bits()).astype(low_precision)
    grad_layer = after(grad_layer, small_core)
    grad_down = grad_layer[:, side_width:].reshape(action_down.shape)
    grad_gate_up = swap_out(grad_layer[:, :side_width], unit_groups)
    grad_out_att = hand_out(grad_out_att, far_bits(), small_plane)
    small_grads = hand_out(small_plane, far_bits())
    for bit in row_bits():
        grad_qkv = halve(grad_qkv, bit, 1, small_plane)
    grad_qkv = hand_out(grad_qkv, far_bits(), small_grads)
    small_grads = unpack_rows(small_grads[None], small_shapes)
    grad_kv, grad_in, grad_head, grad_gains = (part[0] for part in small_grads)
    gradients = (
        grad_gains,
        grad_kv,
        grad_in,
        grad_qkv,
        grad_out_att,
        grad_gate_up.astype(jnp.float32),
        grad_down.astype(jnp.float32),
        grad_head,
    )
    local_squares = sum((jnp.sum(grad_one * grad_one) for grad_one in gradients))
    sums = total(jnp.stack([loss_local, local_squares]))
    loss_sum = sums[0]
    grad_norm = jnp.sqrt(sums[1])
    clip_factor = jnp.minimum(1.0, CLIP_AT / (grad_norm + 1e-06))
    step_rates = (GAIN_RATE,) + (MATRIX_RATE,) * 7
    decay_rates = (0.0,) + (WEIGHT_DECAY,) * 7
    updated = []
    for master_w, moment_one, moment_two, gradient, step_rate, decay_rate in zip(
        masters, moments_one, moments_two, gradients, step_rates, decay_rates
    ):
        updated.extend(
            adamw(master_w, moment_one, moment_two, gradient * clip_factor, step_rate, decay_rate)
        )
    return (
        updated[0],
        updated[1],
        updated[2],
        updated[3],
        updated[4],
        updated[5],
        updated[6],
        updated[7],
        updated[8],
        updated[9],
        updated[10],
        updated[11],
        updated[12],
        updated[13],
        updated[14],
        updated[15],
        updated[16],
        updated[17],
        updated[18],
        updated[19],
        updated[20],
        updated[21],
        updated[22],
        updated[23],
        loss_sum,
        counted,
        grad_norm,
    )


def solution(mesh):
    wide, act = mesh.devices.shape
    lanes_mesh = Mesh(mesh.devices.reshape(wide, act // 2, 2), AXES)
    placed = (
        P(AXES, None),
        P("wide", None),
        P(AXES, None, None),
        P(AXES, None, None),
        P(AXES),
        P(AXES),
        P(AXES),
        P(AXES),
        P(AXES),
        P(AXES, None),
        P(AXES, None),
        P(AXES, None),
        P(AXES, None),
        P(AXES, None),
        P(AXES, None),
        P(AXES, None),
        P(AXES, None),
        P(AXES, None),
        P(AXES, None),
        P(AXES, None),
        P(AXES, None),
        P(AXES, None),
        P(AXES, None),
        P(AXES, None),
        P(AXES, None),
        P(AXES, None),
        P(AXES, None),
        P(AXES, None),
        P(AXES, None),
        P(AXES, None),
    )
    return jax.shard_map(
        on_device,
        mesh=lanes_mesh,
        in_specs=placed,
        out_specs=(
            P(AXES),
            P(AXES),
            P(AXES),
            P(AXES, None),
            P(AXES, None),
            P(AXES, None),
            P(AXES, None),
            P(AXES, None),
            P(AXES, None),
            P(AXES, None),
            P(AXES, None),
            P(AXES, None),
            P(AXES, None),
            P(AXES, None),
            P(AXES, None),
            P(AXES, None),
            P(AXES, None),
            P(AXES, None),
            P(AXES, None),
            P(AXES, None),
            P(AXES, None),
            P(AXES, None),
            P(AXES, None),
            P(AXES, None),
            P(),
            P(),
            P(),
        ),
        check_vma=False,
    )
```
